32 devices in a mesh: row: 4 (over y, x), col: 8 (over z, core).
Axes of the slice: x: 2, y: 2, z: 4, core: 2. Of those that a mesh axis runs over, the one named last changes fastest.
Arguments:
- amplitudes: bfloat16 [8, 8, 512, 512], P('row', None, 'col'), may hold values from -6 to 6
- intermediate: bfloat16 [8, 512, 8, 512], P('row', None, 'col'), may hold values from -0.09375 to 0.09375
Outputs:
- update: bfloat16 [8, 8, 512, 512], P('row', None, 'col')
The draws below stay inside these ranges and needn't reach their ends.
All inputs are finite; a program needn't handle non-finite values.
Results may differ from the reference program's by a relative error of at most 0.0051.
Values may be sent and summed in bfloat16 or wider, within the bound.
No kernel may reach another device: no remote copies, remote signals or barrier semaphores. Data moves between devices by JAX's collectives and lax.ppermute only.
A program may use at most 128 MiB of HBM per device.

```python
import jax
import jax.numpy as jnp
from jax import lax

V = 512
OCC = 8


def levels(rng, shape, pieces, least, top_value):
    level = 1.0
    for position, parts in pieces:
        draws = jax.random.uniform(jax.random.fold_in(jax.random.fold_in(rng, 6), position), (parts,), jnp.float32, least / len(pieces), top_value / len(pieces))
        level = level * jnp.repeat(jnp.exp(draws), shape[position] // parts).reshape((-1,) + (1,) * (len(shape) - 1 - position))
    return level


def scatter_about(own_key, extent, scale, most, split=(), held_as=jnp.bfloat16):
    entries = jax.random.normal(own_key, extent, jnp.float32) * scale
    if len(split) > 0:
        entries = levels(own_key, extent, split, -0.22, 0.18) * entries
    return jnp.clip(entries, min=-most, max=most).astype(held_as)


def setup_inputs(seed: int = 0) -> dict:
    key_list = jax.random.split(jax.random.key(seed), 3)
    amplitudes = scatter_about(key_list[0], (OCC, OCC, V, V), 1.0, 6.0, ((0, 4), (2, 8)))
    intermediate = scatter_about(key_list[1], (OCC, V, OCC, V), (OCC * V) ** -0.5, 0.09375, ((0, 4), (2, 8)))
    return dict(amplitudes=amplitudes, intermediate=intermediate)


def reference(amplitudes, intermediate):
    panel = jnp.transpose(amplitudes, (1, 3, 0, 2)).reshape(OCC * V, OCC * V).astype(jnp.float32)
    weights = intermediate.reshape(OCC * V, OCC * V).astype(jnp.float32)
    cycle = jnp.dot(panel, weights, precision=lax.Precision.HIGHEST, preferred_element_type=jnp.float32)
    cycle = cycle.astype(jnp.bfloat16).reshape(OCC, V, OCC, V)
    first = jnp.transpose(cycle, (0, 2, 1, 3)).astype(jnp.float32)
    second = jnp.transpose(cycle, (2, 0, 3, 1)).astype(jnp.float32)
    return (first + second).astype(jnp.bfloat16)
```

```python
import jax
import jax.numpy as jnp
from jax import lax
from jax.sharding import PartitionSpec as P


def swap_cores(x, ncol):
    return lax.ppermute(x, "col", [(s, s ^ 1) for s in range(ncol)])


def solution(mesh):
    nrow, ncol = mesh.shape["row"], mesh.shape["col"]

    def local(amplitudes, intermediate):
        kk, occ, cs, v = amplitudes.shape
        ai = occ // nrow
        vs = v // ncol
        row = lax.axis_index("row")
        core = lax.axis_index("col") % 2

        w = intermediate[:, :, 0, :]
        own = lax.dynamic_index_in_dim(w, core, 0, keepdims=False)
        other = swap_cores(lax.dynamic_index_in_dim(w, 1 - core, 0, keepdims=False), ncol)
        gathered = []
        for q in range(2):
            part = jnp.where(core == q, own, other)
            g = lax.all_gather(part, "col", axis=0, tiled=False)
            gathered.append(g.reshape(ncol // 2, kk, v, v))

        blocks = amplitudes.reshape(kk, occ, cs, ncol, vs)
        blocks = jnp.transpose(blocks, (3, 0, 2, 1, 4)).reshape(ncol, kk, cs, occ * vs)
        panel = lax.all_to_all(blocks, "col", 0, 0, tiled=True)
        panel = jnp.transpose(panel, (1, 0, 2, 3)).reshape(kk, v, nrow, ai * vs)

        firsts, seconds = [], []
        for q in range(2):
            total = None
            for t in range(nrow):
                mine = lax.dynamic_index_in_dim(panel, row ^ t, 2, keepdims=False)
                part = jnp.einsum(
                    "kcm,jkcb->mjb", mine, gathered[q], preferred_element_type=jnp.float32
                )
                if t > 0:
                    part = lax.ppermute(
                        part.astype(jnp.bfloat16), "row", [(r, r ^ t) for r in range(nrow)]
                    ).astype(jnp.float32)
                total = part if total is None else total + part
            first = total.astype(jnp.bfloat16)
            firsts.append(first)
            turned = jnp.transpose(first, (1, 2, 0)).reshape(nrow * ncol, vs, ai * vs)
            seconds.append(lax.all_to_all(turned, ("row", "col"), 0, 0, tiled=True))

        first = jnp.stack([f.reshape(ai, vs, nrow, v) for f in firsts], 0)
        first = jnp.transpose(first, (1, 3, 0, 2, 4)).reshape(ai, occ, vs, v)
        second = jnp.stack(
            [s.reshape(nrow, ncol, vs, ai, vs).transpose(0, 3, 2, 1, 4) for s in seconds], 0
        ).reshape(ai, occ, vs, v)
        return (first.astype(jnp.float32) + second.astype(jnp.float32)).astype(jnp.bfloat16)

    placed = P("row", None, "col", None)
    return jax.shard_map(
        local, mesh=mesh, in_specs=(placed, placed), out_specs=placed, check_vma=False
    )
```

```python
import jax
import jax.numpy as jnp
from jax import lax
from jax.sharding import PartitionSpec as P

F32, BF16 = jnp.float32, jnp.bfloat16


def solution(mesh):
    nrow, ncol = mesh.shape["row"], mesh.shape["col"]
    nz = ncol // 2
    half = nz // 2

    def across(x):
        return lax.ppermute(x, "col", [(s, s ^ 1) for s in range(ncol)])

    def along(x, pairs):
        both = [(2 * a + c, 2 * b + c) for a, b in pairs for c in range(2)]
        return lax.ppermute(x, "col", both)

    def local(amplitudes, intermediate):
        kk, occ, cs, v = amplitudes.shape
        ai = occ // nrow
        vs = v // ncol
        rows = ai * vs
        row = lax.axis_index("row")
        col = lax.axis_index("col")
        z, core = col // 2, col % 2

        def by_core(x):
            return [lax.dynamic_index_in_dim(x, c, 0, keepdims=False) for c in (core, 1 - core)]

        w = intermediate[:, :, 0, :]
        mine, theirs = by_core(w), by_core(across(w))
        own = [[jnp.where(core == q, a, b) for a, b in zip(mine, theirs)] for q in range(2)]

        blocks = amplitudes.reshape(kk, occ, cs, ncol, vs)
        blocks = jnp.transpose(blocks, (3, 0, 2, 1, 4)).reshape(ncol, kk, cs, occ * vs)
        panel = lax.all_to_all(blocks, "col", 0, 0, tiled=True)
        panel = jnp.transpose(panel, (1, 0, 2, 3)).reshape(kk, v, nrow, rows)
        panel = jnp.stack(by_core(panel), 0)
        panel = [lax.dynamic_index_in_dim(panel, row ^ t, 2, keepdims=False) for t in range(nrow)]

        def product(parts):
            mats = jnp.stack([jnp.stack(p, 0) for p in parts], 0)
            total = None
            sent = []
            for t in range(1, nrow):
                part = jnp.einsum("kcm,nkcb->nmb", panel[t], mats, preferred_element_type=F32)
                sent.append(
                    lax.ppermute(part.astype(BF16), "row", [(r, r ^ t) for r in range(nrow)])
                )
            total = jnp.einsum("kcm,nkcb->nmb", panel[0], mats, preferred_element_type=F32)
            for s in sent:
                total = total + s.astype(F32)
            return total.astype(BF16)

        firsts, seconds = [], []
        for q in range(2):
            arrivals = [(z, own[q])]
            up = down = merged = own[q][0]
            for t in range(1, nz):
                if t < half:
                    up = along(up, [(a, a + 1) for a in range(t - 1, nz - 1)])
                    down = along(down, [(a, a - 1) for a in range(1, nz - t + 1)])
                    arrivals.append((jnp.where(z >= t, z - t, nz), [up, across(up)]))
                    arrivals.append((jnp.where(z < nz - t, z + t, nz), [down, across(down)]))
                    continue
                if t == half:
                    up = along(up, [(a, a + 1) for a in range(t - 1, nz - 1)])
                    down = along(down, [(a, a - 1) for a in range(1, nz - t + 1)])
                    merged = jnp.where(z >= t, up, down)
                else:
                    pairs = [(a, a + 1) for a in range(t - 1, nz - 1)]
                    pairs += [(a, a - 1) for a in range(1, nz - t + 1)]
                    merged = along(merged, pairs)
                slot = jnp.where(z >= t, z - t, jnp.where(z < nz - t, z + t, nz))
                arrivals.append((slot, [merged, across(merged)]))
            groups = [arrivals] if q == 0 else [arrivals[:-1], arrivals[-1:]]
            first = jnp.zeros((nz + 1, rows, v), BF16)
            turned = jnp.zeros((nz + 1, v, rows), BF16)
            for group in groups:
                block = product([m for _, m in group])
                flipped = jnp.transpose(block, (0, 2, 1))
                for n, (slot, _) in enumerate(group):
                    first = lax.dynamic_update_index_in_dim(first, block[n], slot, 0)
                    turned = lax.dynamic_update_index_in_dim(turned, flipped[n], slot, 0)
            firsts.append(first[:nz])
            turned = turned[:nz].reshape(nrow * ncol, vs, rows)
            seconds.append(lax.all_to_all(turned, ("row", "col"), 0, 0, tiled=True))

        first = jnp.stack([f.reshape(nrow, ai, vs, v) for f in firsts], 1)
        first = jnp.transpose(first, (2, 0, 1, 3, 4)).reshape(ai, occ, vs, v)
        second = jnp.stack(
            [s.reshape(nrow, ncol, vs, ai, vs).transpose(0, 3, 2, 1, 4) for s in seconds], 0
        ).reshape(ai, occ, vs, v)
        return (first.astype(F32) + second.astype(F32)).astype(BF16)

    placed = P("row", None, "col", None)
    return jax.shard_map(
        local, mesh=mesh, in_specs=(placed, placed), out_specs=placed, check_vma=False
    )
```

```python
import functools

import jax
import jax.numpy as jnp
from jax import lax
from jax.experimental import pallas as pl
from jax.experimental.pallas import tpu as pltpu
from jax.sharding import PartitionSpec as P

F32, BF16 = jnp.float32, jnp.bfloat16
VMEM = pl.BlockSpec(memory_space=pltpu.VMEM)
SMEM = pl.BlockSpec(memory_space=pltpu.SMEM)
PARAMS = pltpu.CompilerParams(vmem_limit_bytes=40 * 1024 * 1024)


def spread_kernel(nrow, ncol, row_ref, a_ref, out_ref):
    kk, occ, _, v = a_ref.shape
    ai, vs = occ // nrow, v // ncol
    for k in range(kk):
        tiles = [a_ref[k, (row_ref[0] ^ t) * ai + i] for t in range(nrow) for i in range(ai)]
        for s in range(ncol):
            piece = [tile[:, s * vs : (s + 1) * vs] for tile in tiles]
            out_ref[s, k] = jnp.concatenate(piece, axis=1)


def product_kernel(count, nrow, flag_ref, panel_ref, *refs):
    blocks, outs = refs[: 2 * count], refs[2 * count :]
    rows = outs[0].shape[1]

    def run(pick):
        for n in range(count):
            prod = jnp.dot(panel_ref[...], blocks[2 * n + pick][...], preferred_element_type=F32)
            outs[0][n] = prod[:rows]
            for t in range(1, nrow):
                outs[t][n] = prod[t * rows : (t + 1) * rows].astype(BF16)

    @pl.when(flag_ref[0] == 1)
    def _():
        run(0)

    @pl.when(flag_ref[0] == 0)
    def _():
        run(1)


def sum_kernel(groups, nrow, slot_ref, *refs):
    first_ref, turned_ref = refs[-2:]
    at = 0
    for g in range(groups):
        parts = refs[g * nrow : (g + 1) * nrow]
        for n in range(parts[0].shape[0]):
            total = parts[0][n]
            for other in parts[1:]:
                total = total + other[n].astype(F32)
            total = total.astype(BF16)
            first_ref[slot_ref[at]] = total
            turned_ref[slot_ref[at]] = total.astype(F32).T.astype(BF16)
            at += 1


def final_kernel(nrow, ncol, first0, first1, second0, second1, out_ref):
    ai, occ, vs, v = out_ref.shape
    firsts, seconds = (first0, first1), (second0, second1)
    for i in range(ai):
        for r in range(nrow):
            tiles = [seconds[i][r * ncol + s].astype(F32) for s in range(ncol)]
            for q in range(ai):
                second = jnp.concatenate([x[:, q * vs : (q + 1) * vs] for x in tiles], axis=1)
                first = firsts[q][r, i * vs : (i + 1) * vs, :].astype(F32)
                out_ref[i, r * ai + q] = (first + second).astype(BF16)


def solution(mesh):
    nrow, ncol = mesh.shape["row"], mesh.shape["col"]
    nz = ncol // 2
    order = []
    for z in range(nz):
        seq = []
        for t in range(1, nz):
            seq += [(t, 1)] if z >= t else []
            seq += [(t, -1)] if z + t < nz else []
        order.append(seq)

    def core_copy(x, p):
        return lax.ppermute(x, "col", [(2 * a + p, 2 * a + 1 - p) for a in range(nz)])

    def along(x, pairs, p):
        return lax.ppermute(x, "col", [(2 * a + p, 2 * b + p) for a, b in pairs])

    def local(amplitudes, intermediate):
        kk, occ, cs, v = amplitudes.shape
        ai = occ // nrow
        vs = v // ncol
        rows = ai * vs
        row = lax.axis_index("row")
        col = lax.axis_index("col")
        z, core = col // 2, col % 2

        w = intermediate.reshape(kk * v, v)
        other = lax.ppermute(w, "col", [(s, s ^ 1) for s in range(ncol)])

        blocks = pl.pallas_call(
            functools.partial(spread_kernel, nrow, ncol),
            out_shape=jax.ShapeDtypeStruct((ncol, kk, cs, occ * vs), BF16),
            in_specs=[SMEM, VMEM],
            out_specs=VMEM,
            compiler_params=PARAMS,
        )(row.reshape(1), amplitudes)
        panel = lax.all_to_all(blocks, "col", 0, 0, tiled=True)
        panel = jnp.transpose(panel, (3, 1, 0, 2)).reshape(nrow * rows, kk * v)

        def product(p, pairs):
            n = len(pairs)
            flag = (core == p).astype(jnp.int32).reshape(1)
            sent = [jax.ShapeDtypeStruct((n, rows, v), BF16)] * (nrow - 1)
            parts = pl.pallas_call(
                functools.partial(product_kernel, n, nrow),
                out_shape=[jax.ShapeDtypeStruct((n, rows, v), F32)] + sent,
                in_specs=[SMEM] + [VMEM] * (1 + 2 * n),
                out_specs=[VMEM] * nrow,
                compiler_params=PARAMS,
            )(flag, panel, *[x for pair in pairs for x in pair])
            return [parts[0]] + [
                lax.ppermute(parts[t], "row", [(r, r ^ t) for r in range(nrow)])
                for t in range(1, nrow)
            ]

        def chain(p, start):
            got = {}
            blocks = []
            up = down = start
            for t in range(1, nz):
                up = along(up, [(a, a + 1) for a in range(t - 1, nz - 1)], p)
                down = along(down, [(a, a - 1) for a in range(1, nz - t + 1)], p)
                got[t, 1], got[t, -1] = up, down
                picks = [seq[t - 1] for seq in order]
                block = got[picks[0]]
                for pick in sorted(set(picks) - {picks[0]}):
                    hit = functools.reduce(
                        jnp.logical_or, [z == a for a in range(nz) if picks[a] == pick]
                    )
                    block = jnp.where(hit, got[pick], block)
                blocks.append((block, core_copy(block, p)))
            return blocks

        def slots():
            table = []
            for seq in order:
                a = len(table)
                table.append([a] + [a - t * d for t, d in seq])
            return jnp.array(table, jnp.int32)[z]

        where = slots()
        firsts, seconds = [], []
        start = w
        for p in range(2):
            arrived = chain(p, start)
            if p == 0:
                start, _ = lax.optimization_barrier((w, arrived[0][1]))
            here = (w, other)
            groups = [product(p, [here, arrived[0]])]
            groups += [product(p, [pair]) for pair in arrived[1:]]
            first, turned = pl.pallas_call(
                functools.partial(sum_kernel, len(groups), nrow),
                out_shape=[
                    jax.ShapeDtypeStruct((nz, rows, v), BF16),
                    jax.ShapeDtypeStruct((nz, v, rows), BF16),
                ],
                in_specs=[SMEM] + [VMEM] * (len(groups) * nrow),
                out_specs=[VMEM] * 2,
                compiler_params=PARAMS,
            )(where, *[x for g in groups for x in g])
            firsts.append(first)
            turned = turned.reshape(nrow * ncol, vs, rows)
            seconds.append(lax.all_to_all(turned, ("row", "col"), 0, 0, tiled=True))

        return pl.pallas_call(
            functools.partial(final_kernel, nrow, ncol),
            out_shape=jax.ShapeDtypeStruct((ai, occ, vs, v), BF16),
            in_specs=[VMEM] * 4,
            out_specs=VMEM,
            compiler_params=PARAMS,
        )(*firsts, *seconds)

    placed = P("row", None, "col", None)
    return jax.shard_map(
        local, mesh=mesh, in_specs=(placed, placed), out_specs=placed, check_vma=False
    )
```

```python
import functools

import jax
import jax.numpy as jnp
from jax import lax
from jax.experimental import pallas as pl
from jax.experimental.pallas import tpu as pltpu
from jax.sharding import PartitionSpec as P

F32, BF16 = jnp.float32, jnp.bfloat16
VMEM = pl.BlockSpec(memory_space=pltpu.VMEM)
SMEM = pl.BlockSpec(memory_space=pltpu.SMEM)
PARAMS = pltpu.CompilerParams(vmem_limit_bytes=16 * 1024 * 1024)


def spread_kernel(ncol, a_ref, out_ref):
    kk, occ, _, v = a_ref.shape
    vs = v // ncol
    for k in range(kk):
        tiles = [a_ref[k, i] for i in range(occ)]
        for s in range(ncol):
            piece = [tile[:, s * vs : (s + 1) * vs] for tile in tiles]
            out_ref[s, k] = jnp.concatenate(piece, axis=1)


def product_kernel(count, core_ref, panel_ref, *refs):
    blocks, out_ref = refs[:-1], refs[-1]
    nrow, _, rows, _ = out_ref.shape
    core = core_ref[0]
    for m in range(count):
        for c in range(2):
            n = 2 * m + (core ^ c)
            block = blocks[2 * m + c]
            prod = jnp.dot(panel_ref[...], block[...], preferred_element_type=F32).astype(BF16)
            for r in range(nrow):
                out_ref[r, n] = prod[r * rows : (r + 1) * rows]


def turn_kernel(groups, ncol, slot_ref, *refs):
    first_ref, turned_ref = refs[-2:]
    vs = turned_ref.shape[2]
    at = 0
    for ref in refs[:groups]:
        for m in range(ref.shape[0] // 2):
            slot = slot_ref[at]
            at += 1
            for p in range(2):
                total = ref[2 * m + p]
                first_ref[2 * slot + p] = total
                turned = total.astype(F32).T.astype(BF16)
                for s in range(ncol):
                    turned_ref[slot * ncol + s, p] = turned[s * vs : (s + 1) * vs]


def final_kernel(nrow, ncol, first_ref, second_ref, out_ref):
    ai, _, vs, _ = out_ref.shape
    for i in range(ai):
        for r in range(nrow):
            tiles = [second_ref[r * ncol + s, i].astype(F32) for s in range(ncol)]
            for q in range(ai):
                second = jnp.concatenate([x[:, q * vs : (q + 1) * vs] for x in tiles], axis=1)
                first = first_ref[r * ai + q, i * vs : (i + 1) * vs, :].astype(F32)
                out_ref[i, r * ai + q] = (first + second).astype(BF16)


def solution(mesh):
    nrow, ncol = mesh.shape["row"], mesh.shape["col"]
    nz = ncol // 2

    def across(x):
        return lax.ppermute(x, "col", [(s, s ^ 1) for s in range(ncol)])

    def along(x, pairs):
        return lax.ppermute(x, "col", [(2 * a + c, 2 * b + c) for a, b in pairs for c in range(2)])

    def after(x, *earlier):
        return lax.optimization_barrier((x, *earlier))[0]

    def local(amplitudes, intermediate):
        kk, occ, cs, v = amplitudes.shape
        ai = occ // nrow
        vs = v // ncol
        rows = ai * vs
        col = lax.axis_index("col")
        z, core = col // 2, (col % 2).reshape(1)
        end = (z == 0) | (z == nz - 1)

        w = intermediate.reshape(kk * v, v)
        line = nz == 4
        if line:
            swap = [(1, 2), (2, 1)]
            outward = [(1, 0), (2, 3)]
            x1 = along(w, [(a, a ^ 1) for a in range(nz)])
            y2 = along(w, swap)
        own = (w, across(w))

        blocks = pl.pallas_call(
            functools.partial(spread_kernel, ncol),
            out_shape=jax.ShapeDtypeStruct((ncol, kk, cs, occ * vs), BF16),
            in_specs=[VMEM],
            out_specs=VMEM,
            compiler_params=PARAMS,
        )(amplitudes)
        panel = lax.all_to_all(blocks, "col", 0, 0, tiled=True)
        panel = jnp.transpose(panel, (3, 1, 0, 2)).reshape(nrow * rows, kk * v)

        def product(pairs):
            n = 2 * len(pairs)
            return pl.pallas_call(
                functools.partial(product_kernel, len(pairs)),
                out_shape=jax.ShapeDtypeStruct((nrow, n, rows, v), BF16),
                in_specs=[SMEM] + [VMEM] * (1 + n),
                out_specs=VMEM,
                compiler_params=PARAMS,
            )(core, panel, *[x for pair in pairs for x in pair])

        def summed(part):
            n = part.shape[1]
            flat = part.reshape(nrow * n * rows, v)
            flat = lax.psum_scatter(flat, "row", scatter_dimension=0, tiled=True)
            return flat.reshape(n, rows, v)

        if line:
            y3 = along(after(x1, blocks), swap)
            e2 = along(after(y2, blocks), outward)
            part = product([own, (x1, across(x1))])
            e3 = along(after(y3, part), outward)
            groups = [summed(part)]
            for inner, outer in ((y2, e2), (y3, e3)):
                x = jnp.where(end, outer, inner)
                groups.append(summed(product([(after(x, groups[-1]), across(x))])))
            slots = [z, z ^ 1, jnp.where(end, z ^ 2, 3 - z), jnp.where(end, 3 - z, z ^ 2)]
        else:
            groups = [summed(product([own]))]
            for m in range(1, nz):
                x = along(w, [(a, a ^ m) for a in range(nz)])
                groups.append(summed(product([(after(x, groups[-1]), across(x))])))
            slots = [z ^ m for m in range(nz)]

        first, turned = pl.pallas_call(
            functools.partial(turn_kernel, len(groups), ncol),
            out_shape=[
                jax.ShapeDtypeStruct((occ, rows, v), BF16),
                jax.ShapeDtypeStruct((nrow * ncol, ai, vs, rows), BF16),
            ],
            in_specs=[SMEM] + [VMEM] * len(groups),
            out_specs=[VMEM] * 2,
            compiler_params=PARAMS,
        )(jnp.stack(slots).astype(jnp.int32), *groups)
        second = lax.all_to_all(turned, ("row", "col"), 0, 0, tiled=True)

        return pl.pallas_call(
            functools.partial(final_kernel, nrow, ncol),
            out_shape=jax.ShapeDtypeStruct((ai, occ, vs, v), BF16),
            in_specs=[VMEM] * 2,
            out_specs=VMEM,
            compiler_params=PARAMS,
        )(first, second)

    placed = P("row", None, "col", None)
    return jax.shard_map(
        local, mesh=mesh, in_specs=(placed, placed), out_specs=placed, check_vma=False
    )
```

```python
import functools

import jax
import jax.numpy as jnp
from jax import lax
from jax.experimental import pallas as pl
from jax.experimental.pallas import tpu as pltpu
from jax.sharding import PartitionSpec as P

F32, BF16 = jnp.float32, jnp.bfloat16
VMEM = pl.BlockSpec(memory_space=pltpu.VMEM)
SMEM = pl.BlockSpec(memory_space=pltpu.SMEM)
PARAMS = pltpu.CompilerParams(vmem_limit_bytes=16 * 1024 * 1024)


def spread_kernel(nrow, ncol, row_ref, a_ref, out_ref):
    kk, occ, _, v = a_ref.shape
    ai, vs = occ // nrow, v // ncol
    for k in range(kk):
        tiles = [a_ref[k, (row_ref[0] ^ t) * ai + i] for t in range(nrow) for i in range(ai)]
        for s in range(ncol):
            piece = [tile[:, s * vs : (s + 1) * vs] for tile in tiles]
            out_ref[s, k] = jnp.concatenate(piece, axis=1)


def product_kernel(count, core_ref, panel_ref, *refs):
    blocks, outs = refs[: 2 * count], refs[2 * count :]
    rows = outs[0].shape[1]
    core = core_ref[0]
    for m in range(count):
        for c in range(2):
            n = 2 * m + (core ^ c)
            prod = jnp.dot(panel_ref[...], blocks[2 * m + c][...], preferred_element_type=F32)
            outs[0][n] = prod[:rows]
            for t in range(1, len(outs)):
                outs[t][n] = prod[t * rows : (t + 1) * rows].astype(BF16)


def turn_kernel(sizes, ncol, slot_ref, *refs):
    first_ref, turned_ref = refs[-2:]
    vs = turned_ref.shape[2]
    at = 0
    for size in sizes:
        parts, refs = refs[:size], refs[size:]
        for m in range(parts[0].shape[0] // 2):
            slot = slot_ref[at]
            at += 1
            for p in range(2):
                total = parts[0][2 * m + p]
                for other in parts[1:]:
                    total = total + other[2 * m + p].astype(F32)
                total = total.astype(BF16)
                first_ref[2 * slot + p] = total
                turned = total.astype(F32).T.astype(BF16)
                for s in range(ncol):
                    turned_ref[slot * ncol + s, p] = turned[s * vs : (s + 1) * vs]


def final_kernel(nrow, ncol, first_ref, second_ref, out_ref):
    ai, _, vs, _ = out_ref.shape
    for i in range(ai):
        for r in range(nrow):
            tiles = [second_ref[r * ncol + s, i].astype(F32) for s in range(ncol)]
            for q in range(ai):
                second = jnp.concatenate([x[:, q * vs : (q + 1) * vs] for x in tiles], axis=1)
                first = first_ref[r * ai + q, i * vs : (i + 1) * vs, :].astype(F32)
                out_ref[i, r * ai + q] = (first + second).astype(BF16)


def solution(mesh):
    nrow, ncol = mesh.shape["row"], mesh.shape["col"]
    nz = ncol // 2

    def across(x):
        return lax.ppermute(x, "col", [(s, s ^ 1) for s in range(ncol)])

    def along(x, pairs):
        return lax.ppermute(x, "col", [(2 * a + c, 2 * b + c) for a, b in pairs for c in range(2)])

    def after(x, *earlier):
        return lax.optimization_barrier((x, *earlier))[0]

    def local(amplitudes, intermediate):
        kk, occ, cs, v = amplitudes.shape
        ai = occ // nrow
        vs = v // ncol
        rows = ai * vs
        row = lax.axis_index("row").reshape(1)
        col = lax.axis_index("col")
        z, core = col // 2, (col % 2).reshape(1)
        end = (z == 0) | (z == nz - 1)

        w = intermediate.reshape(kk * v, v)
        line = nz == 4
        if line:
            swap = [(1, 2), (2, 1)]
            outward = [(1, 0), (2, 3)]
            x1 = along(w, [(a, a ^ 1) for a in range(nz)])
            y2 = along(w, swap)
        own = (w, across(w))

        blocks = pl.pallas_call(
            functools.partial(spread_kernel, nrow, ncol),
            out_shape=jax.ShapeDtypeStruct((ncol, kk, cs, occ * vs), BF16),
            in_specs=[SMEM, VMEM],
            out_specs=VMEM,
            compiler_params=PARAMS,
        )(row, amplitudes)
        panel = lax.all_to_all(blocks, "col", 0, 0, tiled=True)
        panel = jnp.transpose(panel, (3, 1, 0, 2)).reshape(nrow * rows, kk * v)

        def product(pairs):
            n = 2 * len(pairs)
            sent = [jax.ShapeDtypeStruct((n, rows, v), BF16)] * (nrow - 1)
            return pl.pallas_call(
                functools.partial(product_kernel, len(pairs)),
                out_shape=[jax.ShapeDtypeStruct((n, rows, v), F32)] + sent,
                in_specs=[SMEM] + [VMEM] * (1 + n),
                out_specs=[VMEM] * nrow,
                compiler_params=PARAMS,
            )(core, panel, *[x for pair in pairs for x in pair])

        def exchange(parts):
            return [parts[0]] + [
                lax.ppermute(parts[t], "row", [(r, r ^ t) for r in range(nrow)])
                for t in range(1, nrow)
            ]

        def summed(group):
            total = group[0]
            for part in group[1:]:
                total = total + part.astype(F32)
            return total.astype(BF16)

        if line:
            x1, y2, blocks = lax.optimization_barrier((x1, y2, blocks))
            y3, e2 = along(x1, swap), along(y2, outward)
            parts = product([own, (x1, across(x1))])
            groups = [exchange(parts)]
            e3 = along(after(y3, *parts), outward)
            for inner, outer in ((y2, e2), (y3, e3)):
                groups[-1] = [summed(groups[-1])]
                x = jnp.where(end, after(outer, *parts), inner)
                parts = product([(after(x, groups[-1][0]), across(x))])
                groups.append(exchange(parts))
            slots = [z, z ^ 1, jnp.where(end, z ^ 2, 3 - z), jnp.where(end, 3 - z, z ^ 2)]
        else:
            groups = [exchange(product([own]))]
            for m in range(1, nz):
                groups[-1] = [summed(groups[-1])]
                x = along(w, [(a, a ^ m) for a in range(nz)])
                groups.append(exchange(product([(after(x, groups[-1][0]), across(x))])))
            slots = [z ^ m for m in range(nz)]

        sizes = [len(g) for g in groups]
        first, turned = pl.pallas_call(
            functools.partial(turn_kernel, sizes, ncol),
            out_shape=[
                jax.ShapeDtypeStruct((occ, rows, v), BF16),
                jax.ShapeDtypeStruct((nrow * ncol, ai, vs, rows), BF16),
            ],
            in_specs=[SMEM] + [VMEM] * sum(sizes),
            out_specs=[VMEM] * 2,
            compiler_params=PARAMS,
        )(jnp.stack(slots).astype(jnp.int32), *[x for g in groups for x in g])
        second = lax.all_to_all(turned, ("row", "col"), 0, 0, tiled=True)

        return pl.pallas_call(
            functools.partial(final_kernel, nrow, ncol),
            out_shape=jax.ShapeDtypeStruct((ai, occ, vs, v), BF16),
            in_specs=[VMEM] * 2,
            out_specs=VMEM,
            compiler_params=PARAMS,
        )(first, second)

    placed = P("row", None, "col", None)
    return jax.shard_map(
        local, mesh=mesh, in_specs=(placed, placed), out_specs=placed, check_vma=False
    )
```

```python
import functools

import jax
import jax.numpy as jnp
from jax import lax
from jax.experimental import pallas as pl
from jax.experimental.pallas import tpu as pltpu
from jax.sharding import PartitionSpec as P

F32, BF16 = jnp.float32, jnp.bfloat16
VMEM = pl.BlockSpec(memory_space=pltpu.VMEM)
SMEM = pl.BlockSpec(memory_space=pltpu.SMEM)
PARAMS = pltpu.CompilerParams(vmem_limit_bytes=16 * 1024 * 1024)


def spread_kernel(nrow, ncol, row_ref, a_ref, out_ref):
    kk, occ, _, v = a_ref.shape
    ai, vs = occ // nrow, v // ncol
    for k in range(kk):
        tiles = [a_ref[k, (row_ref[0] ^ t) * ai + i] for t in range(nrow) for i in range(ai)]
        for s in range(ncol):
            piece = [tile[:, s * vs : (s + 1) * vs] for tile in tiles]
            out_ref[s, k] = jnp.concatenate(piece, axis=1)


def product_kernel(split, core_ref, panel_ref, here_ref, there_ref, *outs):
    nrow = len(outs) // 2 if split else len(outs)
    rows = outs[0].shape[1]

    def run(order):
        for p, block in enumerate(order):
            prod = jnp.dot(panel_ref[...], block[...], preferred_element_type=F32)
            to, n = (outs[p * nrow : (p + 1) * nrow], 0) if split else (outs, p)
            to[0][n] = prod[:rows]
            for t in range(1, nrow):
                to[t][n] = prod[t * rows : (t + 1) * rows].astype(BF16)

    pl.when(core_ref[0] == 0)(lambda: run((here_ref, there_ref)))
    pl.when(core_ref[0] == 1)(lambda: run((there_ref, here_ref)))


def turn_kernel(p, ncol, count, slot_ref, *refs):
    first_ref, turned_ref = refs[-2:]
    vs = turned_ref.shape[1]
    total = refs[count][0]
    for other in refs[count + 1 : -2]:
        total = total + other[0].astype(F32)
    for m, value in enumerate([ref[p] for ref in refs[:count]] + [total.astype(BF16)]):
        slot = slot_ref[m]
        first_ref[slot] = value
        turned = value.astype(F32).T.astype(BF16)
        for s in range(ncol):
            turned_ref[slot * ncol + s] = turned[s * vs : (s + 1) * vs]


def final_kernel(nrow, ncol, *refs):
    out_ref = refs[-1]
    ai, _, vs, _ = out_ref.shape
    firsts, seconds = refs[:ai], refs[ai:-1]
    for i in range(ai):
        for r in range(nrow):
            tiles = [seconds[i][r * ncol + s].astype(F32) for s in range(ncol)]
            for q in range(ai):
                second = jnp.concatenate([x[:, q * vs : (q + 1) * vs] for x in tiles], axis=1)
                first = firsts[q][r, i * vs : (i + 1) * vs, :].astype(F32)
                out_ref[i, r * ai + q] = (first + second).astype(BF16)


def solution(mesh):
    nrow, ncol = mesh.shape["row"], mesh.shape["col"]
    nz = ncol // 2

    def across(x):
        return lax.ppermute(x, "col", [(s, s ^ 1) for s in range(ncol)])

    def along(x, pairs):
        return lax.ppermute(x, "col", [(2 * a + c, 2 * b + c) for a, b in pairs for c in range(2)])

    def after(x, *earlier):
        return lax.optimization_barrier((x, *earlier))[0]

    def local(amplitudes, intermediate):
        kk, occ, cs, v = amplitudes.shape
        ai = occ // nrow
        vs = v // ncol
        rows = ai * vs
        row = lax.axis_index("row").reshape(1)
        col = lax.axis_index("col")
        z, core = (col // 2).reshape(1), (col % 2).reshape(1)
        end = (z == 0) | (z == nz - 1)

        w = intermediate.reshape(kk * v, v)
        line = nz == 4
        if line:
            swap = [(1, 2), (2, 1)]
            outward = [(1, 0), (2, 3)]
            x1 = along(w, [(a, a ^ 1) for a in range(nz)])
            y2 = along(w, swap)
        own = (w, across(w))

        blocks = pl.pallas_call(
            functools.partial(spread_kernel, nrow, ncol),
            out_shape=jax.ShapeDtypeStruct((ncol, kk, cs, occ * vs), BF16),
            in_specs=[SMEM, VMEM],
            out_specs=VMEM,
            compiler_params=PARAMS,
        )(row, amplitudes)
        panel = lax.all_to_all(blocks, "col", 0, 0, tiled=True)
        panel = jnp.transpose(panel, (3, 1, 0, 2)).reshape(nrow * rows, kk * v)

        def product(here, there, split=False):
            sets, n = (2, 1) if split else (1, 2)
            sent = [jax.ShapeDtypeStruct((n, rows, v), BF16)] * (nrow - 1)
            parts = pl.pallas_call(
                functools.partial(product_kernel, split),
                out_shape=([jax.ShapeDtypeStruct((n, rows, v), F32)] + sent) * sets,
                in_specs=[SMEM] + [VMEM] * 3,
                out_specs=[VMEM] * (nrow * sets),
                compiler_params=PARAMS,
            )(core, panel, here, there)
            return [parts[a * nrow : (a + 1) * nrow] for a in range(sets)]

        def exchange(parts):
            return [parts[0]] + [
                lax.ppermute(parts[t], "row", [(r, r ^ t) for r in range(nrow)])
                for t in range(1, nrow)
            ]

        def summed(parts):
            total = parts[0]
            for part in exchange(parts)[1:]:
                total = total + part.astype(F32)
            return total.astype(BF16)

        if line:
            x1, y2, blocks = lax.optimization_barrier((x1, y2, blocks))
            y3, e2 = along(x1, swap), along(y2, outward)
            sums = [summed(product(*own)[0])]
            sums.append(summed(product(x1, across(x1))[0]))
            e3 = along(after(y3, sums[0]), outward)
            x2 = jnp.where(end, e2, y2)
            parts = product(after(x2, sums[1]), across(x2))[0]
            sums.append(summed(parts))
            x3 = jnp.where(end, after(e3, *parts), y3)
            last = product(after(x3, sums[2]), across(x3), True)
            slots = [z, z ^ 1, jnp.where(end, z ^ 2, 3 - z), jnp.where(end, 3 - z, z ^ 2)]
        else:
            sums = [summed(product(*own)[0])]
            for m in range(1, nz):
                x = along(w, [(a, a ^ m) for a in range(nz)])
                last = product(after(x, sums[-1]), across(x), m == nz - 1)
                if m < nz - 1:
                    sums.append(summed(last[0]))
            slots = [z ^ m for m in range(nz)]
        slots = jnp.concatenate(slots).astype(jnp.int32)

        firsts, seconds = [], []
        for p, group in enumerate(exchange(g) for g in last):
            first, turned = pl.pallas_call(
                functools.partial(turn_kernel, p, ncol, len(sums)),
                out_shape=[
                    jax.ShapeDtypeStruct((nrow, rows, v), BF16),
                    jax.ShapeDtypeStruct((nrow * ncol, vs, rows), BF16),
                ],
                in_specs=[SMEM] + [VMEM] * (len(sums) + nrow),
                out_specs=[VMEM] * 2,
                compiler_params=PARAMS,
            )(slots, *sums, *group)
            firsts.append(first)
            seconds.append(lax.all_to_all(turned, ("row", "col"), 0, 0, tiled=True))

        return pl.pallas_call(
            functools.partial(final_kernel, nrow, ncol),
            out_shape=jax.ShapeDtypeStruct((ai, occ, vs, v), BF16),
            in_specs=[VMEM] * (2 * ai),
            out_specs=VMEM,
            compiler_params=PARAMS,
        )(*firsts, *seconds)

    placed = P("row", None, "col", None)
    return jax.shard_map(
        local, mesh=mesh, in_specs=(placed, placed), out_specs=placed, check_vma=False
    )
```

```python
import functools

import jax
import jax.numpy as jnp
from jax import lax
from jax.experimental import pallas as pl
from jax.experimental.pallas import tpu as pltpu
from jax.sharding import PartitionSpec as P

F32, BF16 = jnp.float32, jnp.bfloat16
VMEM = pl.BlockSpec(memory_space=pltpu.VMEM)
SMEM = pl.BlockSpec(memory_space=pltpu.SMEM)
PARAMS = pltpu.CompilerParams(vmem_limit_bytes=16 * 1024 * 1024)


def spread_kernel(nrow, ncol, row_ref, a_ref, out_ref):
    kk, occ, _, v = a_ref.shape
    ai, vs = occ // nrow, v // ncol
    for k in range(kk):
        tiles = [a_ref[k, (row_ref[0] ^ t) * ai + i] for t in range(nrow) for i in range(ai)]
        for s in range(ncol):
            piece = [tile[:, s * vs : (s + 1) * vs] for tile in tiles]
            out_ref[s, k] = jnp.concatenate(piece, axis=1)


def product_kernel(count, panel_ref, *refs):
    blocks, outs = refs[:count], refs[count:]
    rows = outs[0].shape[1]
    for n, block in enumerate(blocks):
        prod = jnp.dot(panel_ref[...], block[...], preferred_element_type=F32)
        outs[0][n] = prod[:rows]
        for t in range(1, len(outs)):
            outs[t][n] = prod[t * rows : (t + 1) * rows].astype(BF16)


def turn_kernel(half, ncol, count, slot_ref, *refs):
    first_ref, turned_ref = refs[-2:]
    vs = turned_ref.shape[1]
    total = refs[count][0]
    for other in refs[count + 1 : -2]:
        total = total + other[0].astype(F32)
    for m, value in enumerate([ref[half] for ref in refs[:count]] + [total.astype(BF16)]):
        slot = slot_ref[m]
        first_ref[slot] = value
        turned = value.astype(F32).T.astype(BF16)
        for s in range(ncol):
            turned_ref[slot * ncol + s] = turned[s * vs : (s + 1) * vs]


def final_kernel(nrow, ncol, core_ref, *refs):
    out_ref = refs[-1]
    ai, _, vs, _ = out_ref.shape
    firsts, seconds = refs[:ai], refs[ai:-1]

    def run(core):
        for i in range(ai):
            for r in range(nrow):
                tiles = [seconds[i ^ (s % 2)][r * ncol + s].astype(F32) for s in range(ncol)]
                for q in range(ai):
                    second = jnp.concatenate([x[:, q * vs : (q + 1) * vs] for x in tiles], axis=1)
                    first = firsts[q ^ core][r, i * vs : (i + 1) * vs, :].astype(F32)
                    out_ref[i, r * ai + q] = (first + second).astype(BF16)

    for c in range(2):
        pl.when(core_ref[0] == c)(functools.partial(run, c))


def solution(mesh):
    nrow, ncol = mesh.shape["row"], mesh.shape["col"]
    nz = ncol // 2

    def across(x):
        return lax.ppermute(x, "col", [(s, s ^ 1) for s in range(ncol)])

    def along(x, pairs):
        return lax.ppermute(x, "col", [(2 * a + c, 2 * b + c) for a, b in pairs for c in range(2)])

    def after(x, *earlier):
        return lax.optimization_barrier((x, *earlier))[0]

    def local(amplitudes, intermediate):
        kk, occ, cs, v = amplitudes.shape
        ai = occ // nrow
        vs = v // ncol
        rows = ai * vs
        row = lax.axis_index("row").reshape(1)
        col = lax.axis_index("col")
        z, core = (col // 2).reshape(1), (col % 2).reshape(1)
        end = (z == 0) | (z == nz - 1)

        w = intermediate.reshape(kk * v, v)
        line = nz == 4
        if line:
            swap = [(1, 2), (2, 1)]
            outward = [(1, 0), (2, 3)]
            x1 = along(w, [(a, a ^ 1) for a in range(nz)])
            y2 = along(w, swap)
        own = (w, across(w))

        blocks = pl.pallas_call(
            functools.partial(spread_kernel, nrow, ncol),
            out_shape=jax.ShapeDtypeStruct((ncol, kk, cs, occ * vs), BF16),
            in_specs=[SMEM, VMEM],
            out_specs=VMEM,
            compiler_params=PARAMS,
        )(row, amplitudes)
        panel = lax.all_to_all(blocks, "col", 0, 0, tiled=True)
        panel = jnp.transpose(panel, (3, 1, 0, 2)).reshape(nrow * rows, kk * v)

        def product(*given):
            n = len(given)
            sent = [jax.ShapeDtypeStruct((n, rows, v), BF16)] * (nrow - 1)
            return pl.pallas_call(
                functools.partial(product_kernel, n),
                out_shape=[jax.ShapeDtypeStruct((n, rows, v), F32)] + sent,
                in_specs=[VMEM] * (1 + n),
                out_specs=[VMEM] * nrow,
                compiler_params=PARAMS,
            )(panel, *given)

        def exchange(parts):
            return [parts[0]] + [
                lax.ppermute(parts[t], "row", [(r, r ^ t) for r in range(nrow)])
                for t in range(1, nrow)
            ]

        def summed(group):
            total = group[0]
            for part in group[1:]:
                total = total + part.astype(F32)
            return total.astype(BF16)

        if line:
            x1, y2, blocks = lax.optimization_barrier((x1, y2, blocks))
            y3, e2 = along(x1, swap), along(y2, outward)
            group = exchange(product(*own))
            e3 = along(after(y3, *group[1:]), outward)
            sums = [summed(group)]
            sums.append(summed(exchange(product(x1, across(x1)))))
            x2 = jnp.where(end, e2, y2)
            group = exchange(product(after(x2, sums[1]), across(x2)))
            x = jnp.where(end, after(e3, *group[1:]), y3)
            sums.append(summed(group))
            slots = [z, z ^ 1, jnp.where(end, z ^ 2, 3 - z), jnp.where(end, 3 - z, z ^ 2)]
        else:
            sums = [summed(exchange(product(*own)))]
            for m in range(1, nz):
                x = after(along(w, [(a, a ^ m) for a in range(nz)]), sums[-1])
                if m < nz - 1:
                    sums.append(summed(exchange(product(x, across(x)))))
            slots = [z ^ m for m in range(nz)]
        slots = jnp.concatenate(slots).astype(jnp.int32)

        firsts, seconds = [], []
        for half, group in enumerate([exchange(product(x)), exchange(product(across(x)))]):
            first, turned = pl.pallas_call(
                functools.partial(turn_kernel, half, ncol, len(sums)),
                out_shape=[
                    jax.ShapeDtypeStruct((nrow, rows, v), BF16),
                    jax.ShapeDtypeStruct((nrow * ncol, vs, rows), BF16),
                ],
                in_specs=[SMEM] + [VMEM] * (len(sums) + nrow),
                out_specs=[VMEM] * 2,
                compiler_params=PARAMS,
            )(slots, *sums, *group)
            firsts.append(first)
            seconds.append(lax.all_to_all(turned, ("row", "col"), 0, 0, tiled=True))

        return pl.pallas_call(
            functools.partial(final_kernel, nrow, ncol),
            out_shape=jax.ShapeDtypeStruct((ai, occ, vs, v), BF16),
            in_specs=[SMEM] + [VMEM] * (2 * ai),
            out_specs=VMEM,
            compiler_params=PARAMS,
        )(core, *firsts, *seconds)

    placed = P("row", None, "col", None)
    return jax.shard_map(
        local, mesh=mesh, in_specs=(placed, placed), out_specs=placed, check_vma=False
    )
```

```python
import functools

import jax
import jax.numpy as jnp
from jax import lax
from jax.experimental import pallas as pl
from jax.experimental.pallas import tpu as pltpu
from jax.sharding import PartitionSpec as P

F32, BF16 = jnp.float32, jnp.bfloat16
VMEM = pl.BlockSpec(memory_space=pltpu.VMEM)
SMEM = pl.BlockSpec(memory_space=pltpu.SMEM)
PARAMS = pltpu.CompilerParams(vmem_limit_bytes=16 * 1024 * 1024)


def spread_kernel(nrow, ncol, row_ref, a_ref, out_ref):
    kk, occ, _, v = a_ref.shape
    ai, vs = occ // nrow, v // ncol
    for k in range(kk):
        tiles = [a_ref[k, (row_ref[0] ^ t) * ai + i] for t in range(nrow) for i in range(ai)]
        for s in range(ncol):
            piece = [tile[:, s * vs : (s + 1) * vs] for tile in tiles]
            out_ref[s, k] = jnp.concatenate(piece, axis=1)


def product_kernel(count, core_ref, panel_ref, *refs):
    blocks, outs = refs[: 2 * count], refs[2 * count :]
    rows = outs[0].shape[1]
    core = core_ref[0]
    for m in range(count):
        for c in range(2):
            n = 2 * m + (core ^ c)
            prod = jnp.dot(panel_ref[...], blocks[2 * m + c][...], preferred_element_type=F32)
            outs[0][n] = prod[:rows]
            for t in range(1, len(outs)):
                outs[t][n] = prod[t * rows : (t + 1) * rows].astype(BF16)


def turn_kernel(sizes, ncol, slot_ref, *refs):
    first_ref, turned_ref = refs[-2:]
    vs = turned_ref.shape[2]
    at = 0
    for size in sizes:
        parts, refs = refs[:size], refs[size:]
        for m in range(parts[0].shape[0] // 2):
            slot = slot_ref[at]
            at += 1
            for p in range(2):
                total = parts[0][2 * m + p]
                for other in parts[1:]:
                    total = total + other[2 * m + p].astype(F32)
                total = total.astype(BF16)
                first_ref[2 * slot + p] = total
                turned = total.astype(F32).T.astype(BF16)
                for s in range(ncol):
                    turned_ref[slot * ncol + s, p] = turned[s * vs : (s + 1) * vs]


def final_kernel(nrow, ncol, first_ref, second_ref, out_ref):
    ai, _, vs, _ = out_ref.shape
    for i in range(ai):
        for r in range(nrow):
            tiles = [second_ref[r * ncol + s, i].astype(F32) for s in range(ncol)]
            for q in range(ai):
                second = jnp.concatenate([x[:, q * vs : (q + 1) * vs] for x in tiles], axis=1)
                first = first_ref[r * ai + q, i * vs : (i + 1) * vs, :].astype(F32)
                out_ref[i, r * ai + q] = (first + second).astype(BF16)


def solution(mesh):
    nrow, ncol = mesh.shape["row"], mesh.shape["col"]
    nz = ncol // 2

    def across(x):
        return lax.ppermute(x, "col", [(s, s ^ 1) for s in range(ncol)])

    def along(x, pairs):
        return lax.ppermute(x, "col", [(2 * a + c, 2 * b + c) for a, b in pairs for c in range(2)])

    def after(x, *earlier):
        return lax.optimization_barrier((x, *earlier))[0]

    def local(amplitudes, intermediate):
        kk, occ, cs, v = amplitudes.shape
        ai = occ // nrow
        vs = v // ncol
        rows = ai * vs
        row = lax.axis_index("row").reshape(1)
        col = lax.axis_index("col")
        z, core = col // 2, (col % 2).reshape(1)
        end = (z == 0) | (z == nz - 1)

        w = intermediate.reshape(kk * v, v)
        line = nz == 4
        if line:
            swap = [(1, 2), (2, 1)]
            outward = [(1, 0), (2, 3)]
            x1 = along(w, [(a, a ^ 1) for a in range(nz)])
            y2 = along(after(w, x1), swap)
        own = (w, across(w))

        blocks = pl.pallas_call(
            functools.partial(spread_kernel, nrow, ncol),
            out_shape=jax.ShapeDtypeStruct((ncol, kk, cs, occ * vs), BF16),
            in_specs=[SMEM, VMEM],
            out_specs=VMEM,
            compiler_params=PARAMS,
        )(row, amplitudes)
        panel = lax.all_to_all(blocks, "col", 0, 0, tiled=True)
        panel = jnp.transpose(panel, (3, 1, 0, 2)).reshape(nrow * rows, kk * v)

        def product(pairs):
            n = 2 * len(pairs)
            sent = [jax.ShapeDtypeStruct((n, rows, v), BF16)] * (nrow - 1)
            return pl.pallas_call(
                functools.partial(product_kernel, len(pairs)),
                out_shape=[jax.ShapeDtypeStruct((n, rows, v), F32)] + sent,
                in_specs=[SMEM] + [VMEM] * (1 + n),
                out_specs=[VMEM] * nrow,
                compiler_params=PARAMS,
            )(core, panel, *[x for pair in pairs for x in pair])

        def exchange(parts):
            return [parts[0]] + [
                lax.ppermute(parts[t], "row", [(r, r ^ t) for r in range(nrow)])
                for t in range(1, nrow)
            ]

        def summed(group):
            total = group[0]
            for part in group[1:]:
                total = total + part.astype(F32)
            return total.astype(BF16)

        if line:
            x1, y2, blocks = lax.optimization_barrier((x1, y2, blocks))
            y3, e2 = along(x1, swap), along(y2, outward)
            parts = product([own, (x1, across(x1))])
            groups = [exchange(parts)]
            e3 = along(after(y3, *parts), outward)
            for inner, outer in ((y2, e2), (y3, e3)):
                groups[-1] = [summed(groups[-1])]
                x = jnp.where(end, after(outer, *parts), inner)
                parts = product([(after(x, groups[-1][0]), across(x))])
                groups.append(exchange(parts))
            slots = [z, z ^ 1, jnp.where(end, z ^ 2, 3 - z), jnp.where(end, 3 - z, z ^ 2)]
        else:
            groups = [exchange(product([own]))]
            for m in range(1, nz):
                groups[-1] = [summed(groups[-1])]
                x = along(w, [(a, a ^ m) for a in range(nz)])
                groups.append(exchange(product([(after(x, groups[-1][0]), across(x))])))
            slots = [z ^ m for m in range(nz)]

        sizes = [len(g) for g in groups]
        first, turned = pl.pallas_call(
            functools.partial(turn_kernel, sizes, ncol),
            out_shape=[
                jax.ShapeDtypeStruct((occ, rows, v), BF16),
                jax.ShapeDtypeStruct((nrow * ncol, ai, vs, rows), BF16),
            ],
            in_specs=[SMEM] + [VMEM] * sum(sizes),
            out_specs=[VMEM] * 2,
            compiler_params=PARAMS,
        )(jnp.stack(slots).astype(jnp.int32), *[x for g in groups for x in g])
        second = lax.all_to_all(turned, ("row", "col"), 0, 0, tiled=True)

        return pl.pallas_call(
            functools.partial(final_kernel, nrow, ncol),
            out_shape=jax.ShapeDtypeStruct((ai, occ, vs, v), BF16),
            in_specs=[VMEM] * 2,
            out_specs=VMEM,
            compiler_params=PARAMS,
        )(first, second)

    placed = P("row", None, "col", None)
    return jax.shard_map(
        local, mesh=mesh, in_specs=(placed, placed), out_specs=placed, check_vma=False
    )
```

```python
import functools

import jax
import jax.numpy as jnp
from jax import lax
from jax.experimental import pallas as pl
from jax.experimental.pallas import tpu as pltpu
from jax.sharding import PartitionSpec as P

F32, BF16 = jnp.float32, jnp.bfloat16
VMEM = pl.BlockSpec(memory_space=pltpu.VMEM)
SMEM = pl.BlockSpec(memory_space=pltpu.SMEM)
PARAMS = pltpu.CompilerParams(vmem_limit_bytes=16 * 1024 * 1024)


def spread_kernel(nrow, ncol, row_ref, a_ref, out_ref):
    kk, occ, _, v = a_ref.shape
    ai, vs = occ // nrow, v // ncol
    for k in range(kk):
        tiles = [a_ref[k, (row_ref[0] ^ t) * ai + i] for t in range(nrow) for i in range(ai)]
        for s in range(ncol):
            piece = [tile[:, s * vs : (s + 1) * vs] for tile in tiles]
            out_ref[s, k] = jnp.concatenate(piece, axis=1)


def product_kernel(sets, core_ref, panel_ref, *refs):
    core = core_ref[0]
    blocks, outs = refs[: 2 * sets], refs[2 * sets :]
    size = len(outs) // sets
    rows = outs[0].shape[1]
    for m in range(sets):
        to = outs[m * size : (m + 1) * size]
        for c in range(2):
            prod = jnp.dot(panel_ref[...], blocks[2 * m + c][...], preferred_element_type=F32)
            to[0][core ^ c] = prod[:rows]
            for t in range(1, size):
                to[t][core ^ c] = prod[t * rows : (t + 1) * rows].astype(BF16)


def turn_kernel(sizes, ncol, slot_ref, *refs):
    first_ref, turned_ref = refs[-2:]
    vs = turned_ref.shape[2]
    at = 0
    for size in sizes:
        parts, refs = refs[:size], refs[size:]
        for m in range(parts[0].shape[0] // 2):
            slot = slot_ref[at]
            at += 1
            for p in range(2):
                total = parts[0][2 * m + p]
                for other in parts[1:]:
                    total = total + other[2 * m + p].astype(F32)
                total = total.astype(BF16)
                first_ref[2 * slot + p] = total
                turned = total.astype(F32).T.astype(BF16)
                for s in range(ncol):
                    turned_ref[slot * ncol + s, p] = turned[s * vs : (s + 1) * vs]


def final_kernel(nrow, ncol, first_ref, second_ref, out_ref):
    ai, _, vs, _ = out_ref.shape
    for i in range(ai):
        for r in range(nrow):
            tiles = [second_ref[r * ncol + s, i].astype(F32) for s in range(ncol)]
            for q in range(ai):
                second = jnp.concatenate([x[:, q * vs : (q + 1) * vs] for x in tiles], axis=1)
                first = first_ref[r * ai + q, i * vs : (i + 1) * vs, :].astype(F32)
                out_ref[i, r * ai + q] = (first + second).astype(BF16)


def solution(mesh):
    nrow, ncol = mesh.shape["row"], mesh.shape["col"]
    nz = ncol // 2

    def across(x):
        return lax.ppermute(x, "col", [(s, s ^ 1) for s in range(ncol)])

    def along(x, pairs):
        return lax.ppermute(x, "col", [(2 * a + c, 2 * b + c) for a, b in pairs for c in range(2)])

    def after(x, *earlier):
        return lax.optimization_barrier((x, *earlier))[0]

    def local(amplitudes, intermediate):
        kk, occ, cs, v = amplitudes.shape
        ai = occ // nrow
        vs = v // ncol
        rows = ai * vs
        row = lax.axis_index("row").reshape(1)
        col = lax.axis_index("col")
        z, core = col // 2, (col % 2).reshape(1)
        end = (z == 0) | (z == nz - 1)

        w = intermediate.reshape(kk * v, v)
        line = nz == 4
        if line:
            swap = [(1, 2), (2, 1)]
            outward = [(1, 0), (2, 3)]
            x1 = along(w, [(a, a ^ 1) for a in range(nz)])
            y2 = along(w, swap)
        own = (w, across(w))

        blocks = pl.pallas_call(
            functools.partial(spread_kernel, nrow, ncol),
            out_shape=jax.ShapeDtypeStruct((ncol, kk, cs, occ * vs), BF16),
            in_specs=[SMEM, VMEM],
            out_specs=VMEM,
            compiler_params=PARAMS,
        )(row, amplitudes)
        panel = lax.all_to_all(blocks, "col", 0, 0, tiled=True)
        panel = jnp.transpose(panel, (3, 1, 0, 2)).reshape(nrow * rows, kk * v)

        def product(*pairs):
            sets = len(pairs)
            sent = [jax.ShapeDtypeStruct((2, rows, v), BF16)] * (nrow - 1)
            parts = pl.pallas_call(
                functools.partial(product_kernel, sets),
                out_shape=([jax.ShapeDtypeStruct((2, rows, v), F32)] + sent) * sets,
                in_specs=[SMEM] + [VMEM] * (1 + 2 * sets),
                out_specs=[VMEM] * (nrow * sets),
                compiler_params=PARAMS,
            )(core, panel, *[x for pair in pairs for x in pair])
            return [parts[m * nrow : (m + 1) * nrow] for m in range(sets)]

        def exchange(parts):
            return [parts[0]] + [
                lax.ppermute(parts[t], "row", [(r, r ^ t) for r in range(nrow)])
                for t in range(1, nrow)
            ]

        def summed(group):
            total = group[0]
            for part in group[1:]:
                total = total + part.astype(F32)
            return total.astype(BF16)

        if line:
            x1, y2, blocks = lax.optimization_barrier((x1, y2, blocks))
            y3, e2 = along(x1, swap), along(y2, outward)
            parts, parts1 = product(own, (x1, across(x1)))
            sums = [summed(exchange(parts))]
            e3 = along(after(y3, sums[0]), outward)
            sums.append(summed(exchange(parts1)))
            x2 = jnp.where(end, e2, y2)
            group = exchange(product((after(x2, sums[1]), across(x2)))[0])
            sums.append(summed(group))
            x3 = jnp.where(end, after(e3, *group[1:]), y3)
            last = exchange(product((x3, across(x3)))[0])
            slots = [z, z ^ 1, jnp.where(end, z ^ 2, 3 - z), jnp.where(end, 3 - z, z ^ 2)]
        else:
            last = exchange(product(own)[0])
            sums = []
            for m in range(1, nz):
                sums.append(summed(last))
                x = along(w, [(a, a ^ m) for a in range(nz)])
                last = exchange(product((after(x, sums[-1]), across(x)))[0])
            slots = [z ^ m for m in range(nz)]
        groups = [[x] for x in sums] + [last]

        sizes = [len(g) for g in groups]
        first, turned = pl.pallas_call(
            functools.partial(turn_kernel, sizes, ncol),
            out_shape=[
                jax.ShapeDtypeStruct((occ, rows, v), BF16),
                jax.ShapeDtypeStruct((nrow * ncol, ai, vs, rows), BF16),
            ],
            in_specs=[SMEM] + [VMEM] * sum(sizes),
            out_specs=[VMEM] * 2,
            compiler_params=PARAMS,
        )(jnp.stack(slots).astype(jnp.int32), *[x for g in groups for x in g])
        second = lax.all_to_all(turned, ("row", "col"), 0, 0, tiled=True)

        return pl.pallas_call(
            functools.partial(final_kernel, nrow, ncol),
            out_shape=jax.ShapeDtypeStruct((ai, occ, vs, v), BF16),
            in_specs=[VMEM] * 2,
            out_specs=VMEM,
            compiler_params=PARAMS,
        )(first, second)

    placed = P("row", None, "col", None)
    return jax.shard_map(
        local, mesh=mesh, in_specs=(placed, placed), out_specs=placed, check_vma=False
    )
```

```python
import functools

import jax
import jax.numpy as jnp
from jax import lax
from jax.experimental import pallas as pl
from jax.experimental.pallas import tpu as pltpu
from jax.sharding import PartitionSpec as P

F32, BF16 = jnp.float32, jnp.bfloat16
VMEM = pl.BlockSpec(memory_space=pltpu.VMEM)
SMEM = pl.BlockSpec(memory_space=pltpu.SMEM)
PARAMS = pltpu.CompilerParams(vmem_limit_bytes=16 * 1024 * 1024)


def spread_kernel(nrow, ncol, row_ref, a_ref, out_ref):
    kk, occ, _, v = a_ref.shape
    ai, vs = occ // nrow, v // ncol
    for k in range(kk):
        tiles = [a_ref[k, (row_ref[0] ^ t) * ai + i] for t in range(nrow) for i in range(ai)]
        for s in range(ncol):
            piece = [tile[:, s * vs : (s + 1) * vs] for tile in tiles]
            out_ref[s, k] = jnp.concatenate(piece, axis=1)


def product_kernel(sets, core_ref, panel_ref, *refs):
    core = core_ref[0]
    blocks, outs = refs[: 2 * sets], refs[2 * sets :]
    size = len(outs) // sets
    rows = outs[0].shape[1]
    for m in range(sets):
        to = outs[m * size : (m + 1) * size]
        for c in range(2):
            prod = jnp.dot(panel_ref[...], blocks[2 * m + c][...], preferred_element_type=F32)
            to[0][core ^ c] = prod[:rows]
            for t in range(1, size):
                to[t][core ^ c] = prod[t * rows : (t + 1) * rows].astype(BF16)


def first_product_kernel(core_ref, raw_ref, here_ref, there_ref, panel_ref, *outs):
    ncol, kk, cs, wide = raw_ref.shape
    v = ncol * cs
    for k in range(kk):
        part = raw_ref[:, k].reshape(v, wide)
        panel_ref[:, k * v : (k + 1) * v] = part.T
    product_kernel(1, core_ref, panel_ref, here_ref, there_ref, *outs)


def turn_kernel(sizes, ncol, slot_ref, *refs):
    first_ref, turned_ref = refs[-2:]
    vs = turned_ref.shape[2]
    at = 0
    for size in sizes:
        parts, refs = refs[:size], refs[size:]
        for m in range(parts[0].shape[0] // 2):
            slot = slot_ref[at]
            at += 1
            for p in range(2):
                total = parts[0][2 * m + p]
                for other in parts[1:]:
                    total = total + other[2 * m + p].astype(F32)
                total = total.astype(BF16)
                first_ref[2 * slot + p] = total
                turned = total.astype(F32).T.astype(BF16)
                for s in range(ncol):
                    turned_ref[slot * ncol + s, p] = turned[s * vs : (s + 1) * vs]


def final_kernel(nrow, ncol, first_ref, second_ref, out_ref):
    ai, _, vs, _ = out_ref.shape
    for i in range(ai):
        for r in range(nrow):
            tiles = [second_ref[r * ncol + s, i].astype(F32) for s in range(ncol)]
            for q in range(ai):
                second = jnp.concatenate([x[:, q * vs : (q + 1) * vs] for x in tiles], axis=1)
                first = first_ref[r * ai + q, i * vs : (i + 1) * vs, :].astype(F32)
                out_ref[i, r * ai + q] = (first + second).astype(BF16)


def solution(mesh):
    nrow, ncol = mesh.shape["row"], mesh.shape["col"]
    nz = ncol // 2

    def across(x):
        return lax.ppermute(x, "col", [(s, s ^ 1) for s in range(ncol)])

    def along(x, pairs):
        return lax.ppermute(x, "col", [(2 * a + c, 2 * b + c) for a, b in pairs for c in range(2)])

    def after(x, *earlier):
        return lax.optimization_barrier((x, *earlier))[0]

    def local(amplitudes, intermediate):
        kk, occ, cs, v = amplitudes.shape
        ai = occ // nrow
        vs = v // ncol
        rows = ai * vs
        row = lax.axis_index("row").reshape(1)
        col = lax.axis_index("col")
        z, core = col // 2, (col % 2).reshape(1)
        end = (z == 0) | (z == nz - 1)

        w = intermediate.reshape(kk * v, v)
        line = nz == 4
        own = (w, across(w))
        if line:
            swap = [(1, 2), (2, 1)]
            outward = [(1, 0), (2, 3)]
            x1 = along(w, [(a, a ^ 1) for a in range(nz)])
            y2 = along(w, swap)
            pair1 = (x1, across(x1))
            own = (w, after(own[1], pair1[1]))

        blocks = pl.pallas_call(
            functools.partial(spread_kernel, nrow, ncol),
            out_shape=jax.ShapeDtypeStruct((ncol, kk, cs, occ * vs), BF16),
            in_specs=[SMEM, VMEM],
            out_specs=VMEM,
            compiler_params=PARAMS,
        )(row, amplitudes)
        raw = lax.all_to_all(blocks, "col", 0, 0, tiled=True)
        sent = [jax.ShapeDtypeStruct((2, rows, v), BF16)] * (nrow - 1)
        sent = [jax.ShapeDtypeStruct((2, rows, v), F32)] + sent
        panel, *parts = pl.pallas_call(
            first_product_kernel,
            out_shape=[jax.ShapeDtypeStruct((nrow * rows, kk * v), BF16)] + sent,
            in_specs=[SMEM] + [VMEM] * 3,
            out_specs=[VMEM] * (1 + nrow),
            compiler_params=PARAMS,
        )(core, raw, *own)

        def product(pair):
            return pl.pallas_call(
                functools.partial(product_kernel, 1),
                out_shape=sent,
                in_specs=[SMEM] + [VMEM] * 3,
                out_specs=[VMEM] * nrow,
                compiler_params=PARAMS,
            )(core, panel, *pair)

        def exchange(parts):
            return [parts[0]] + [
                lax.ppermute(parts[t], "row", [(r, r ^ t) for r in range(nrow)])
                for t in range(1, nrow)
            ]

        def summed(group):
            total = group[0]
            for part in group[1:]:
                total = total + part.astype(F32)
            return total.astype(BF16)

        if line:
            x1, y2, blocks = lax.optimization_barrier((x1, y2, blocks))
            y3, e2 = along(x1, swap), along(y2, outward)
            sums = [summed(exchange(parts))]
            parts = product(pair1)
            e3 = along(after(y3, sums[0], *parts), outward)
            sums.append(summed(exchange(parts)))
            x2 = jnp.where(end, e2, y2)
            group = exchange(product((after(x2, sums[1]), across(x2))))
            sums.append(summed(group))
            x3 = jnp.where(end, after(e3, *group[1:]), y3)
            last = exchange(product((x3, across(x3))))
            slots = [z, z ^ 1, jnp.where(end, z ^ 2, 3 - z), jnp.where(end, 3 - z, z ^ 2)]
        else:
            last = exchange(parts)
            sums = []
            for m in range(1, nz):
                sums.append(summed(last))
                x = along(w, [(a, a ^ m) for a in range(nz)])
                last = exchange(product((after(x, sums[-1]), across(x))))
            slots = [z ^ m for m in range(nz)]
        groups = [[x] for x in sums] + [last]

        sizes = [len(g) for g in groups]
        first, turned = pl.pallas_call(
            functools.partial(turn_kernel, sizes, ncol),
            out_shape=[
                jax.ShapeDtypeStruct((occ, rows, v), BF16),
                jax.ShapeDtypeStruct((nrow * ncol, ai, vs, rows), BF16),
            ],
            in_specs=[SMEM] + [VMEM] * sum(sizes),
            out_specs=[VMEM] * 2,
            compiler_params=PARAMS,
        )(jnp.stack(slots).astype(jnp.int32), *[x for g in groups for x in g])
        second = lax.all_to_all(turned, ("row", "col"), 0, 0, tiled=True)

        return pl.pallas_call(
            functools.partial(final_kernel, nrow, ncol),
            out_shape=jax.ShapeDtypeStruct((ai, occ, vs, v), BF16),
            in_specs=[VMEM] * 2,
            out_specs=VMEM,
            compiler_params=PARAMS,
        )(first, second)

    placed = P("row", None, "col", None)
    return jax.shard_map(
        local, mesh=mesh, in_specs=(placed, placed), out_specs=placed, check_vma=False
    )
```

```python
import functools

import jax
import jax.numpy as jnp
from jax import lax
from jax.experimental import pallas as pl
from jax.experimental.pallas import tpu as pltpu
from jax.sharding import PartitionSpec as P

F32, BF16 = jnp.float32, jnp.bfloat16
VMEM = pl.BlockSpec(memory_space=pltpu.VMEM)
SMEM = pl.BlockSpec(memory_space=pltpu.SMEM)
PARAMS = pltpu.CompilerParams(vmem_limit_bytes=16 * 1024 * 1024)


def spread_kernel(nrow, ncol, row_ref, a_ref, *out_refs):
    kk, occ, _, v = a_ref.shape
    ai, vs = occ // nrow, v // ncol
    for odd, out_ref in enumerate(out_refs):
        for k in range(kk):
            tiles = [
                a_ref[k, (row_ref[0] ^ t) * ai + i] for t in range(odd, nrow, 2) for i in range(ai)
            ]
            for s in range(ncol):
                piece = [tile[:, s * vs : (s + 1) * vs] for tile in tiles]
                out_ref[s, k] = jnp.concatenate(piece, axis=1)


def multiply(core, panel_ref, blocks, outs):
    rows = outs[0].shape[1]
    for m, block in enumerate(blocks):
        n = m - m % 2 + ((m % 2) ^ core)
        prod = jnp.dot(panel_ref[...], block[...], preferred_element_type=F32)
        for o, out in enumerate(outs):
            out[n] = prod[o * rows : (o + 1) * rows].astype(out.dtype)


def opening_kernel(count, core_ref, raw_ref, *refs):
    panel_ref = refs[count]
    ncol, kk, cs, wide = raw_ref.shape
    v = ncol * cs
    for k in range(kk):
        panel_ref[:, k * v : (k + 1) * v] = raw_ref[:, k].reshape(v, wide).T
    multiply(core_ref[0], panel_ref, refs[:count], refs[count + 1 :])


def product_kernel(core_ref, even_ref, odd_ref, here_ref, there_ref, *outs):
    half = len(outs) // 2
    for panel_ref, part in ((even_ref, outs[:half]), (odd_ref, outs[half:])):
        multiply(core_ref[0], panel_ref, (here_ref, there_ref), part)


def turn_kernel(sizes, ncol, slot_ref, *refs):
    first_ref, turned_ref = refs[-2:]
    vs = turned_ref.shape[2]
    at = 0
    for size in sizes:
        parts, refs = refs[:size], refs[size:]
        for m in range(parts[0].shape[0] // 2):
            slot = slot_ref[at]
            at += 1
            for p in range(2):
                total = parts[0][2 * m + p]
                for other in parts[1:]:
                    total = total + other[2 * m + p].astype(F32)
                total = total.astype(BF16)
                first_ref[2 * slot + p] = total
                turned = total.astype(F32).T.astype(BF16)
                for s in range(ncol):
                    turned_ref[slot * ncol + s, p] = turned[s * vs : (s + 1) * vs]


def final_kernel(nrow, ncol, first_ref, second_ref, out_ref):
    ai, _, vs, _ = out_ref.shape
    for i in range(ai):
        for r in range(nrow):
            tiles = [second_ref[r * ncol + s, i].astype(F32) for s in range(ncol)]
            for q in range(ai):
                second = jnp.concatenate([x[:, q * vs : (q + 1) * vs] for x in tiles], axis=1)
                first = first_ref[r * ai + q, i * vs : (i + 1) * vs, :].astype(F32)
                out_ref[i, r * ai + q] = (first + second).astype(BF16)


def solution(mesh):
    nrow, ncol = mesh.shape["row"], mesh.shape["col"]
    nz = ncol // 2

    def across(x):
        return lax.ppermute(x, "col", [(s, s ^ 1) for s in range(ncol)])

    def along(x, pairs):
        return lax.ppermute(x, "col", [(2 * a + c, 2 * b + c) for a, b in pairs for c in range(2)])

    def after(x, *earlier):
        return lax.optimization_barrier((x, *earlier))[0]

    def local(amplitudes, intermediate):
        kk, occ, cs, v = amplitudes.shape
        ai = occ // nrow
        vs = v // ncol
        rows = ai * vs
        row = lax.axis_index("row").reshape(1)
        col = lax.axis_index("col")
        z, core = col // 2, (col % 2).reshape(1)
        end = (z == 0) | (z == nz - 1)

        w = intermediate.reshape(kk * v, v)
        line = nz == 4
        first_blocks = [w, across(w)]
        if line:
            swap = [(1, 2), (2, 1)]
            outward = [(1, 0), (2, 3)]
            x1 = along(w, [(a, a ^ 1) for a in range(nz)])
            y2 = along(w, swap)
            first_blocks += [x1, across(x1)]

        wide = occ * vs // 2
        even, odd = pl.pallas_call(
            functools.partial(spread_kernel, nrow, ncol),
            out_shape=[jax.ShapeDtypeStruct((ncol, kk, cs, wide), BF16)] * 2,
            in_specs=[SMEM, VMEM],
            out_specs=[VMEM] * 2,
            compiler_params=PARAMS,
        )(row, amplitudes)

        def shapes(n, kinds):
            return [jax.ShapeDtypeStruct((n, rows, v), kind) for kind in kinds]

        def opening(raw, kinds):
            count = len(first_blocks)
            panel, *parts = pl.pallas_call(
                functools.partial(opening_kernel, count),
                out_shape=[jax.ShapeDtypeStruct((wide, kk * v), BF16)] + shapes(count, kinds),
                in_specs=[SMEM] + [VMEM] * (1 + count),
                out_specs=[VMEM] * (1 + len(kinds)),
                compiler_params=PARAMS,
            )(core, raw, *first_blocks)
            return panel, parts

        half = nrow // 2
        kinds = [F32] + [BF16] * (half - 1)

        def product(here, there):
            return pl.pallas_call(
                product_kernel,
                out_shape=shapes(2, kinds + [BF16] * half),
                in_specs=[SMEM] + [VMEM] * 4,
                out_specs=[VMEM] * nrow,
                compiler_params=PARAMS,
            )(core, even, odd, here, there)

        def to_owner(parts, start):
            return [
                lax.ppermute(part, "row", [(r, r ^ (start + 2 * n)) for r in range(nrow)])
                for n, part in enumerate(parts)
            ]

        def exchange(parts):
            return [parts[0]] + to_owner(parts[1:half], 2) + to_owner(parts[half:], 1)

        def summed(group):
            total = group[0]
            for part in group[1:]:
                total = total + part.astype(F32)
            return total.astype(BF16)

        odd = lax.all_to_all(odd, "col", 0, 0, tiled=True)
        if line:
            x1, y2, odd = lax.optimization_barrier((x1, y2, odd))
            y3, e2 = along(x1, swap), along(y2, outward)
        even = lax.all_to_all(after(even, odd), "col", 0, 0, tiled=True)
        odd, parts = opening(odd, [BF16] * half)
        odd_sums = to_owner(parts, 1)
        even, parts = opening(even, kinds)
        sums = [summed([parts[0]] + to_owner(parts[1:], 2) + odd_sums)]
        if line:
            e3 = along(after(y3, *odd_sums, *parts), outward)
            x2 = jnp.where(end, e2, y2)
            group = exchange(product(after(x2, sums[0]), across(x2)))
            sums.append(summed(group))
            x3 = jnp.where(end, after(e3, *group[1:]), y3)
            last = exchange(product(x3, across(x3)))
            slots = [z, z ^ 1, jnp.where(end, z ^ 2, 3 - z), jnp.where(end, 3 - z, z ^ 2)]
        else:
            for m in range(1, nz):
                x = along(w, [(a, a ^ m) for a in range(nz)])
                last = exchange(product(after(x, sums[-1]), across(x)))
                if m < nz - 1:
                    sums.append(summed(last))
            slots = [z ^ m for m in range(nz)]
        groups = [[x] for x in sums] + [last]

        sizes = [len(g) for g in groups]
        first, turned = pl.pallas_call(
            functools.partial(turn_kernel, sizes, ncol),
            out_shape=[
                jax.ShapeDtypeStruct((occ, rows, v), BF16),
                jax.ShapeDtypeStruct((nrow * ncol, ai, vs, rows), BF16),
            ],
            in_specs=[SMEM] + [VMEM] * sum(sizes),
            out_specs=[VMEM] * 2,
            compiler_params=PARAMS,
        )(jnp.stack(slots).astype(jnp.int32), *[x for g in groups for x in g])
        second = lax.all_to_all(turned, ("row", "col"), 0, 0, tiled=True)

        return pl.pallas_call(
            functools.partial(final_kernel, nrow, ncol),
            out_shape=jax.ShapeDtypeStruct((ai, occ, vs, v), BF16),
            in_specs=[VMEM] * 2,
            out_specs=VMEM,
            compiler_params=PARAMS,
        )(first, second)

    placed = P("row", None, "col", None)
    return jax.shard_map(
        local, mesh=mesh, in_specs=(placed, placed), out_specs=placed, check_vma=False
    )
```

```python
import functools

import jax
import jax.numpy as jnp
from jax import lax
from jax.experimental import pallas as pl
from jax.experimental.pallas import tpu as pltpu
from jax.sharding import PartitionSpec as P

F32, BF16 = jnp.float32, jnp.bfloat16
VMEM = pl.BlockSpec(memory_space=pltpu.VMEM)
SMEM = pl.BlockSpec(memory_space=pltpu.SMEM)
PARAMS = pltpu.CompilerParams(vmem_limit_bytes=16 * 1024 * 1024)


def spread_kernel(nrow, ncol, row_ref, a_ref, out_ref):
    kk, occ, _, v = a_ref.shape
    ai, vs = occ // nrow, v // ncol
    for k in range(kk):
        tiles = [a_ref[k, (row_ref[0] ^ t) * ai + i] for t in range(nrow) for i in range(ai)]
        for s in range(ncol):
            piece = [tile[:, s * vs : (s + 1) * vs] for tile in tiles]
            out_ref[s, k] = jnp.concatenate(piece, axis=1)


def product_kernel(sets, core_ref, panel_ref, *refs):
    core = core_ref[0]
    blocks, outs = refs[: 2 * sets], refs[2 * sets :]
    size = len(outs) // sets
    rows = outs[0].shape[1]
    for m in range(sets):
        to = outs[m * size : (m + 1) * size]
        for c in range(2):
            prod = jnp.dot(panel_ref[...], blocks[2 * m + c][...], preferred_element_type=F32)
            to[0][core ^ c] = prod[:rows]
            for t in range(1, size):
                to[t][core ^ c] = prod[t * rows : (t + 1) * rows].astype(BF16)


def first_product_kernel(core_ref, raw_ref, here_ref, there_ref, panel_ref, *outs):
    ncol, kk, cs, wide = raw_ref.shape
    v = ncol * cs
    for k in range(kk):
        part = raw_ref[:, k].reshape(v, wide)
        panel_ref[:, k * v : (k + 1) * v] = part.T
    product_kernel(1, core_ref, panel_ref, here_ref, there_ref, *outs)


def turn_kernel(sizes, ncol, slot_ref, *refs):
    first_ref, turned_ref = refs[-2:]
    vs = turned_ref.shape[2]
    at = 0
    for size in sizes:
        parts, refs = refs[:size], refs[size:]
        for m in range(parts[0].shape[0] // 2):
            slot = slot_ref[at]
            at += 1
            for p in range(2):
                total = parts[0][2 * m + p]
                for other in parts[1:]:
                    total = total + other[2 * m + p].astype(F32)
                total = total.astype(BF16)
                first_ref[2 * slot + p] = total
                turned = total.astype(F32).T.astype(BF16)
                for s in range(ncol):
                    turned_ref[slot * ncol + s, p] = turned[s * vs : (s + 1) * vs]


def final_kernel(nrow, ncol, first_ref, second_ref, out_ref):
    ai, _, vs, _ = out_ref.shape
    for i in range(ai):
        for r in range(nrow):
            tiles = [second_ref[r * ncol + s, i].astype(F32) for s in range(ncol)]
            for q in range(ai):
                second = jnp.concatenate([x[:, q * vs : (q + 1) * vs] for x in tiles], axis=1)
                first = first_ref[r * ai + q, i * vs : (i + 1) * vs, :].astype(F32)
                out_ref[i, r * ai + q] = (first + second).astype(BF16)


def solution(mesh):
    nrow, ncol = mesh.shape["row"], mesh.shape["col"]
    nz = ncol // 2

    def across(x):
        return lax.ppermute(x, "col", [(s, s ^ 1) for s in range(ncol)])

    def along(x, pairs):
        return lax.ppermute(x, "col", [(2 * a + c, 2 * b + c) for a, b in pairs for c in range(2)])

    def after(x, *earlier):
        return lax.optimization_barrier((x, *earlier))[0]

    def local(amplitudes, intermediate):
        kk, occ, cs, v = amplitudes.shape
        ai = occ // nrow
        vs = v // ncol
        rows = ai * vs
        row = lax.axis_index("row").reshape(1)
        col = lax.axis_index("col")
        z, core = col // 2, (col % 2).reshape(1)
        end = (z == 0) | (z == nz - 1)

        w = intermediate.reshape(kk * v, v)
        line = nz == 4
        own = (w, across(w))
        if line:
            swap = [(1, 2), (2, 1)]
            outward = [(1, 0), (2, 3)]
            x1 = along(w, [(a, a ^ 1) for a in range(nz)])
            y2 = along(w, swap)
            pair1 = (x1, across(x1))
            own = (w, after(own[1], pair1[1]))

        blocks = pl.pallas_call(
            functools.partial(spread_kernel, nrow, ncol),
            out_shape=jax.ShapeDtypeStruct((ncol, kk, cs, occ * vs), BF16),
            in_specs=[SMEM, VMEM],
            out_specs=VMEM,
            compiler_params=PARAMS,
        )(row, amplitudes)
        raw = lax.all_to_all(blocks, "col", 0, 0, tiled=True)
        sent = [jax.ShapeDtypeStruct((2, rows, v), BF16)] * (nrow - 1)
        sent = [jax.ShapeDtypeStruct((2, rows, v), F32)] + sent
        panel, *parts = pl.pallas_call(
            first_product_kernel,
            out_shape=[jax.ShapeDtypeStruct((nrow * rows, kk * v), BF16)] + sent,
            in_specs=[SMEM] + [VMEM] * 3,
            out_specs=[VMEM] * (1 + nrow),
            compiler_params=PARAMS,
        )(core, raw, *own)

        def product(pair):
            return pl.pallas_call(
                functools.partial(product_kernel, 1),
                out_shape=sent,
                in_specs=[SMEM] + [VMEM] * 3,
                out_specs=[VMEM] * nrow,
                compiler_params=PARAMS,
            )(core, panel, *pair)

        def exchange(parts):
            return [parts[0]] + [
                lax.ppermute(parts[t], "row", [(r, r ^ t) for r in range(nrow)])
                for t in range(1, nrow)
            ]

        def summed(group):
            total = group[0]
            for part in group[1:]:
                total = total + part.astype(F32)
            return total.astype(BF16)

        if line:
            x1, y2, blocks = lax.optimization_barrier((x1, y2, blocks))
            y3, e2 = along(x1, swap), along(y2, outward)
            sums = [summed(exchange(parts))]
            parts = product(pair1)
            group = exchange(parts)
            e3 = along(after(y3, sums[0], group[-1]), outward)
            sums.append(summed(group))
            x2 = jnp.where(end, e2, y2)
            group = exchange(product((after(x2, sums[1]), across(x2))))
            sums.append(summed(group))
            x3 = jnp.where(end, after(e3, group[-1]), y3)
            last = exchange(product((x3, across(x3))))
            slots = [z, z ^ 1, jnp.where(end, z ^ 2, 3 - z), jnp.where(end, 3 - z, z ^ 2)]
        else:
            last = exchange(parts)
            sums = []
            for m in range(1, nz):
                sums.append(summed(last))
                x = along(w, [(a, a ^ m) for a in range(nz)])
                last = exchange(product((after(x, sums[-1]), across(x))))
            slots = [z ^ m for m in range(nz)]
        groups = [[x] for x in sums] + [last]

        sizes = [len(g) for g in groups]
        first, turned = pl.pallas_call(
            functools.partial(turn_kernel, sizes, ncol),
            out_shape=[
                jax.ShapeDtypeStruct((occ, rows, v), BF16),
                jax.ShapeDtypeStruct((nrow * ncol, ai, vs, rows), BF16),
            ],
            in_specs=[SMEM] + [VMEM] * sum(sizes),
            out_specs=[VMEM] * 2,
            compiler_params=PARAMS,
        )(jnp.stack(slots).astype(jnp.int32), *[x for g in groups for x in g])
        second = lax.all_to_all(turned, ("row", "col"), 0, 0, tiled=True)

        return pl.pallas_call(
            functools.partial(final_kernel, nrow, ncol),
            out_shape=jax.ShapeDtypeStruct((ai, occ, vs, v), BF16),
            in_specs=[VMEM] * 2,
            out_specs=VMEM,
            compiler_params=PARAMS,
        )(first, second)

    placed = P("row", None, "col", None)
    return jax.shard_map(
        local, mesh=mesh, in_specs=(placed, placed), out_specs=placed, check_vma=False
    )
```

```python
import functools

import jax
import jax.numpy as jnp
from jax import lax
from jax.experimental import pallas as pl
from jax.experimental.pallas import tpu as pltpu
from jax.sharding import PartitionSpec as P

F32, BF16 = jnp.float32, jnp.bfloat16
VMEM = pl.BlockSpec(memory_space=pltpu.VMEM)
SMEM = pl.BlockSpec(memory_space=pltpu.SMEM)
PARAMS = pltpu.CompilerParams(vmem_limit_bytes=16 * 1024 * 1024)


def spread_kernel(nrow, ncol, row_ref, a_ref, out_ref):
    kk, occ, _, v = a_ref.shape
    ai, vs = occ // nrow, v // ncol
    for k in range(kk):
        tiles = [a_ref[k, (row_ref[0] ^ t) * ai + i] for t in range(nrow) for i in range(ai)]
        for s in range(ncol):
            piece = [tile[:, s * vs : (s + 1) * vs] for tile in tiles]
            out_ref[s, k] = jnp.concatenate(piece, axis=1)


def product_kernel(sets, core_ref, panel_ref, *refs):
    core = core_ref[0]
    blocks, outs = refs[: 2 * sets], refs[2 * sets :]
    size = len(outs) // sets
    rows = outs[0].shape[1]
    for m in range(sets):
        to = outs[m * size : (m + 1) * size]
        for c in range(2):
            prod = jnp.dot(panel_ref[...], blocks[2 * m + c][...], preferred_element_type=F32)
            to[0][core ^ c] = prod[:rows]
            for t in range(1, size):
                to[t][core ^ c] = prod[t * rows : (t + 1) * rows].astype(BF16)


def first_product_kernel(core_ref, raw_ref, here_ref, there_ref, panel_ref, *outs):
    ncol, kk, cs, wide = raw_ref.shape
    v = ncol * cs
    for k in range(kk):
        part = raw_ref[:, k].reshape(v, wide)
        panel_ref[:, k * v : (k + 1) * v] = part.T
    product_kernel(1, core_ref, panel_ref, here_ref, there_ref, *outs)


def turn_kernel(sizes, ncol, slot_ref, *refs):
    first_ref, turned_ref = refs[-2:]
    vs = turned_ref.shape[2]
    at = 0
    for size in sizes:
        parts, refs = refs[:size], refs[size:]
        for m in range(parts[0].shape[0] // 2):
            slot = slot_ref[at]
            at += 1
            for p in range(2):
                total = parts[0][2 * m + p]
                for other in parts[1:]:
                    total = total + other[2 * m + p].astype(F32)
                total = total.astype(BF16)
                first_ref[2 * slot + p] = total
                turned = total.astype(F32).T.astype(BF16)
                for s in range(ncol):
                    turned_ref[slot * ncol + s, p] = turned[s * vs : (s + 1) * vs]


def final_kernel(nrow, ncol, first_ref, second_ref, out_ref):
    ai, _, vs, _ = out_ref.shape
    for i in range(ai):
        for r in range(nrow):
            tiles = [second_ref[r * ncol + s, i].astype(F32) for s in range(ncol)]
            for q in range(ai):
                second = jnp.concatenate([x[:, q * vs : (q + 1) * vs] for x in tiles], axis=1)
                first = first_ref[r * ai + q, i * vs : (i + 1) * vs, :].astype(F32)
                out_ref[i, r * ai + q] = (first + second).astype(BF16)


def solution(mesh):
    nrow, ncol = mesh.shape["row"], mesh.shape["col"]
    nz = ncol // 2

    def across(x):
        return lax.ppermute(x, "col", [(s, s ^ 1) for s in range(ncol)])

    def along(x, pairs):
        return lax.ppermute(x, "col", [(2 * a + c, 2 * b + c) for a, b in pairs for c in range(2)])

    def after(x, *earlier):
        return lax.optimization_barrier((x, *earlier))[0]

    def local(amplitudes, intermediate):
        kk, occ, cs, v = amplitudes.shape
        ai = occ // nrow
        vs = v // ncol
        rows = ai * vs
        row = lax.axis_index("row").reshape(1)
        col = lax.axis_index("col")
        z, core = col // 2, (col % 2).reshape(1)
        end = (z == 0) | (z == nz - 1)

        w = intermediate.reshape(kk * v, v)
        line = nz == 4
        own = (w, across(w))
        if line:
            swap = [(1, 2), (2, 1)]
            outward = [(1, 0), (2, 3)]
            x1 = along(w, [(a, a ^ 1) for a in range(nz)])
            y2 = along(w, swap)
            pair1 = (x1, across(x1))
            own = (w, after(own[1], pair1[1]))

        blocks = pl.pallas_call(
            functools.partial(spread_kernel, nrow, ncol),
            out_shape=jax.ShapeDtypeStruct((ncol, kk, cs, occ * vs), BF16),
            in_specs=[SMEM, VMEM],
            out_specs=VMEM,
            compiler_params=PARAMS,
        )(row, amplitudes)
        raw = lax.all_to_all(blocks, "col", 0, 0, tiled=True)
        sent = [jax.ShapeDtypeStruct((2, rows, v), BF16)] * (nrow - 1)
        sent = [jax.ShapeDtypeStruct((2, rows, v), F32)] + sent
        panel, *parts = pl.pallas_call(
            first_product_kernel,
            out_shape=[jax.ShapeDtypeStruct((nrow * rows, kk * v), BF16)] + sent,
            in_specs=[SMEM] + [VMEM] * 3,
            out_specs=[VMEM] * (1 + nrow),
            compiler_params=PARAMS,
        )(core, raw, *own)

        def product(pair):
            return pl.pallas_call(
                functools.partial(product_kernel, 1),
                out_shape=sent,
                in_specs=[SMEM] + [VMEM] * 3,
                out_specs=[VMEM] * nrow,
                compiler_params=PARAMS,
            )(core, panel, *pair)

        def exchange(parts):
            return [parts[0]] + [
                lax.ppermute(parts[t], "row", [(r, r ^ t) for r in range(nrow)])
                for t in range(1, nrow)
            ]

        def summed(group):
            total = group[0]
            for part in group[1:]:
                total = total + part.astype(F32)
            return total.astype(BF16)

        if line:
            x1, y2, blocks = lax.optimization_barrier((x1, y2, blocks))
            y3, e2 = along(x1, swap), along(y2, outward)
            sums = [summed(exchange(parts))]
            parts = product(pair1)
            group = exchange(parts)
            e3 = along(after(y3, sums[0], group[-1]), outward)
            sums.append(summed(group))
            x2 = jnp.where(end, e2, y2)
            group = exchange(product((after(x2, sums[1]), across(x2))))
            sums.append(summed(group))
            x3 = jnp.where(end, after(e3, *group[nrow // 2 :]), y3)
            last = exchange(product((x3, across(x3))))
            slots = [z, z ^ 1, jnp.where(end, z ^ 2, 3 - z), jnp.where(end, 3 - z, z ^ 2)]
        else:
            last = exchange(parts)
            sums = []
            for m in range(1, nz):
                sums.append(summed(last))
                x = along(w, [(a, a ^ m) for a in range(nz)])
                last = exchange(product((after(x, sums[-1]), across(x))))
            slots = [z ^ m for m in range(nz)]
        groups = [[x] for x in sums] + [last]

        sizes = [len(g) for g in groups]
        first, turned = pl.pallas_call(
            functools.partial(turn_kernel, sizes, ncol),
            out_shape=[
                jax.ShapeDtypeStruct((occ, rows, v), BF16),
                jax.ShapeDtypeStruct((nrow * ncol, ai, vs, rows), BF16),
            ],
            in_specs=[SMEM] + [VMEM] * sum(sizes),
            out_specs=[VMEM] * 2,
            compiler_params=PARAMS,
        )(jnp.stack(slots).astype(jnp.int32), *[x for g in groups for x in g])
        second = lax.all_to_all(turned, ("row", "col"), 0, 0, tiled=True)

        return pl.pallas_call(
            functools.partial(final_kernel, nrow, ncol),
            out_shape=jax.ShapeDtypeStruct((ai, occ, vs, v), BF16),
            in_specs=[VMEM] * 2,
            out_specs=VMEM,
            compiler_params=PARAMS,
        )(first, second)

    placed = P("row", None, "col", None)
    return jax.shard_map(
        local, mesh=mesh, in_specs=(placed, placed), out_specs=placed, check_vma=False
    )
```

```python
import functools

import jax
import jax.numpy as jnp
from jax import lax
from jax.experimental import pallas as pl
from jax.experimental.pallas import tpu as pltpu
from jax.sharding import PartitionSpec as P

F32, BF16 = jnp.float32, jnp.bfloat16
VMEM = pl.BlockSpec(memory_space=pltpu.VMEM)
SMEM = pl.BlockSpec(memory_space=pltpu.SMEM)
PARAMS = pltpu.CompilerParams(vmem_limit_bytes=16 * 1024 * 1024)


def spread_kernel(nrow, ncol, row_ref, a_ref, out_ref):
    kk, occ, _, v = a_ref.shape
    ai, vs = occ // nrow, v // ncol
    for k in range(kk):
        tiles = [a_ref[k, (row_ref[0] ^ t) * ai + i] for t in range(nrow) for i in range(ai)]
        for s in range(ncol):
            piece = [tile[:, s * vs : (s + 1) * vs] for tile in tiles]
            out_ref[s, k] = jnp.concatenate(piece, axis=1)


def product_kernel(sets, core_ref, panel_ref, *refs):
    core = core_ref[0]
    blocks, outs = refs[: 2 * sets], refs[2 * sets :]
    size = len(outs) // sets
    rows = outs[0].shape[1]
    for m in range(sets):
        to = outs[m * size : (m + 1) * size]
        for c in range(2):
            prod = jnp.dot(panel_ref[...], blocks[2 * m + c][...], preferred_element_type=F32)
            to[0][core ^ c] = prod[:rows]
            for t in range(1, size):
                to[t][core ^ c] = prod[t * rows : (t + 1) * rows].astype(BF16)


def first_product_kernel(core_ref, raw_ref, here_ref, there_ref, panel_ref, *outs):
    ncol, kk, cs, wide = raw_ref.shape
    v = ncol * cs
    for k in range(kk):
        part = raw_ref[:, k].reshape(v, wide)
        panel_ref[:, k * v : (k + 1) * v] = part.T
    product_kernel(1, core_ref, panel_ref, here_ref, there_ref, *outs)


def turn_kernel(sizes, ncol, slot_ref, *refs):
    first_ref, turned_ref = refs[-2:]
    vs = turned_ref.shape[2]
    at = 0
    for size in sizes:
        parts, refs = refs[:size], refs[size:]
        for m in range(parts[0].shape[0] // 2):
            slot = slot_ref[at]
            at += 1
            for p in range(2):
                total = parts[0][2 * m + p]
                for other in parts[1:]:
                    total = total + other[2 * m + p].astype(F32)
                total = total.astype(BF16)
                first_ref[2 * slot + p] = total
                turned = total.astype(F32).T.astype(BF16)
                for s in range(ncol):
                    turned_ref[slot * ncol + s, p] = turned[s * vs : (s + 1) * vs]


def final_kernel(nrow, ncol, first_ref, second_ref, out_ref):
    ai, _, vs, _ = out_ref.shape
    for i in range(ai):
        for r in range(nrow):
            tiles = [second_ref[r * ncol + s, i].astype(F32) for s in range(ncol)]
            for q in range(ai):
                second = jnp.concatenate([x[:, q * vs : (q + 1) * vs] for x in tiles], axis=1)
                first = first_ref[r * ai + q, i * vs : (i + 1) * vs, :].astype(F32)
                out_ref[i, r * ai + q] = (first + second).astype(BF16)


def solution(mesh):
    nrow, ncol = mesh.shape["row"], mesh.shape["col"]
    nz = ncol // 2

    def across(x):
        return lax.ppermute(x, "col", [(s, s ^ 1) for s in range(ncol)])

    def along(x, pairs):
        return lax.ppermute(x, "col", [(2 * a + c, 2 * b + c) for a, b in pairs for c in range(2)])

    def after(x, *earlier):
        return lax.optimization_barrier((x, *earlier))[0]

    def local(amplitudes, intermediate):
        kk, occ, cs, v = amplitudes.shape
        ai = occ // nrow
        vs = v // ncol
        rows = ai * vs
        row = lax.axis_index("row").reshape(1)
        col = lax.axis_index("col")
        z, core = col // 2, (col % 2).reshape(1)
        end = (z == 0) | (z == nz - 1)

        w = intermediate.reshape(kk * v, v)
        line = nz == 4
        own = (w, across(w))
        if line:
            swap = [(1, 2), (2, 1)]
            outward = [(1, 0), (2, 3)]
            x1 = along(w, [(a, a ^ 1) for a in range(nz)])
            y2 = along(w, swap)
            pair1 = (x1, across(x1))
            own = (w, after(own[1], pair1[1]))

        blocks = pl.pallas_call(
            functools.partial(spread_kernel, nrow, ncol),
            out_shape=jax.ShapeDtypeStruct((ncol, kk, cs, occ * vs), BF16),
            in_specs=[SMEM, VMEM],
            out_specs=VMEM,
            compiler_params=PARAMS,
        )(row, amplitudes)
        raw = lax.all_to_all(blocks, "col", 0, 0, tiled=True)
        sent = [jax.ShapeDtypeStruct((2, rows, v), BF16)] * (nrow - 1)
        sent = [jax.ShapeDtypeStruct((2, rows, v), F32)] + sent
        panel, *parts = pl.pallas_call(
            first_product_kernel,
            out_shape=[jax.ShapeDtypeStruct((nrow * rows, kk * v), BF16)] + sent,
            in_specs=[SMEM] + [VMEM] * 3,
            out_specs=[VMEM] * (1 + nrow),
            compiler_params=PARAMS,
        )(core, raw, *own)

        def product(pair):
            return pl.pallas_call(
                functools.partial(product_kernel, 1),
                out_shape=sent,
                in_specs=[SMEM] + [VMEM] * 3,
                out_specs=[VMEM] * nrow,
                compiler_params=PARAMS,
            )(core, panel, *pair)

        def exchange(parts):
            sent = {}
            for t in range(nrow - 1, 0, -1):
                sent[t] = lax.ppermute(parts[t], "row", [(r, r ^ t) for r in range(nrow)])
            return [parts[0]] + [sent[t] for t in range(1, nrow)]

        def summed(group):
            total = group[0]
            for part in group[1:]:
                total = total + part.astype(F32)
            return total.astype(BF16)

        if line:
            x1, y2, blocks = lax.optimization_barrier((x1, y2, blocks))
            y3, e2 = along(x1, swap), along(y2, outward)
            sums = [summed(exchange(parts))]
            parts = product(pair1)
            group = exchange(parts)
            e3 = along(after(y3, sums[0], group[-1]), outward)
            sums.append(summed(group))
            x2 = jnp.where(end, e2, y2)
            group = exchange(product((after(x2, sums[1]), across(x2))))
            sums.append(summed(group))
            x3 = jnp.where(end, after(e3, *group[nrow // 2 :]), y3)
            last = exchange(product((x3, across(x3))))
            last = [last[0]] + last[:0:-1]
            slots = [z, z ^ 1, jnp.where(end, z ^ 2, 3 - z), jnp.where(end, 3 - z, z ^ 2)]
        else:
            last = exchange(parts)
            sums = []
            for m in range(1, nz):
                sums.append(summed(last))
                x = along(w, [(a, a ^ m) for a in range(nz)])
                last = exchange(product((after(x, sums[-1]), across(x))))
            slots = [z ^ m for m in range(nz)]
        groups = [[x] for x in sums] + [last]

        sizes = [len(g) for g in groups]
        first, turned = pl.pallas_call(
            functools.partial(turn_kernel, sizes, ncol),
            out_shape=[
                jax.ShapeDtypeStruct((occ, rows, v), BF16),
                jax.ShapeDtypeStruct((nrow * ncol, ai, vs, rows), BF16),
            ],
            in_specs=[SMEM] + [VMEM] * sum(sizes),
            out_specs=[VMEM] * 2,
            compiler_params=PARAMS,
        )(jnp.stack(slots).astype(jnp.int32), *[x for g in groups for x in g])
        second = lax.all_to_all(turned, ("row", "col"), 0, 0, tiled=True)

        return pl.pallas_call(
            functools.partial(final_kernel, nrow, ncol),
            out_shape=jax.ShapeDtypeStruct((ai, occ, vs, v), BF16),
            in_specs=[VMEM] * 2,
            out_specs=VMEM,
            compiler_params=PARAMS,
        )(first, second)

    placed = P("row", None, "col", None)
    return jax.shard_map(
        local, mesh=mesh, in_specs=(placed, placed), out_specs=placed, check_vma=False
    )
```

```python
import functools

import jax
import jax.numpy as jnp
from jax import lax
from jax.experimental import pallas as pl
from jax.experimental.pallas import tpu as pltpu
from jax.sharding import PartitionSpec as P

F32, BF16 = jnp.float32, jnp.bfloat16
VMEM = pl.BlockSpec(memory_space=pltpu.VMEM)
SMEM = pl.BlockSpec(memory_space=pltpu.SMEM)
PARAMS = pltpu.CompilerParams(vmem_limit_bytes=16 * 1024 * 1024)


def spread_kernel(nrow, ncol, row_ref, a_ref, out_ref):
    kk, occ, _, v = a_ref.shape
    ai, vs = occ // nrow, v // ncol
    for k in range(kk):
        tiles = [a_ref[k, (row_ref[0] ^ t) * ai + i] for t in range(nrow) for i in range(ai)]
        for s in range(ncol):
            piece = [tile[:, s * vs : (s + 1) * vs] for tile in tiles]
            out_ref[s, k] = jnp.concatenate(piece, axis=1)


def product_kernel(sets, core_ref, panel_ref, *refs):
    core = core_ref[0]
    blocks, outs = refs[: 2 * sets], refs[2 * sets :]
    size = len(outs) // sets
    rows = outs[0].shape[1]
    for m in range(sets):
        to = outs[m * size : (m + 1) * size]
        for c in range(2):
            prod = jnp.dot(panel_ref[...], blocks[2 * m + c][...], preferred_element_type=F32)
            to[0][core ^ c] = prod[:rows]
            for t in range(1, size):
                to[t][core ^ c] = prod[t * rows : (t + 1) * rows].astype(BF16)


def first_product_kernel(core_ref, raw_ref, here_ref, there_ref, panel_ref, *outs):
    ncol, kk, cs, wide = raw_ref.shape
    v = ncol * cs
    for k in range(kk):
        part = raw_ref[:, k].reshape(v, wide)
        panel_ref[:, k * v : (k + 1) * v] = part.T
    product_kernel(1, core_ref, panel_ref, here_ref, there_ref, *outs)


def turn_kernel(sizes, ncol, slot_ref, *refs):
    first_ref, turned_ref = refs[-2:]
    vs = turned_ref.shape[2]
    at = 0
    for size in sizes:
        parts, refs = refs[:size], refs[size:]
        for m in range(parts[0].shape[0] // 2):
            slot = slot_ref[at]
            at += 1
            for p in range(2):
                total = parts[0][2 * m + p]
                for other in parts[1:]:
                    total = total + other[2 * m + p].astype(F32)
                total = total.astype(BF16)
                first_ref[2 * slot + p] = total
                turned = total.astype(F32).T.astype(BF16)
                for s in range(ncol):
                    turned_ref[slot * ncol + s, p] = turned[s * vs : (s + 1) * vs]


def final_kernel(nrow, ncol, first_ref, second_ref, out_ref):
    ai, _, vs, _ = out_ref.shape
    for i in range(ai):
        for r in range(nrow):
            tiles = [second_ref[r * ncol + s, i].astype(F32) for s in range(ncol)]
            for q in range(ai):
                second = jnp.concatenate([x[:, q * vs : (q + 1) * vs] for x in tiles], axis=1)
                first = first_ref[r * ai + q, i * vs : (i + 1) * vs, :].astype(F32)
                out_ref[i, r * ai + q] = (first + second).astype(BF16)


def solution(mesh):
    nrow, ncol = mesh.shape["row"], mesh.shape["col"]
    nz = ncol // 2

    def across(x):
        return lax.ppermute(x, "col", [(s, s ^ 1) for s in range(ncol)])

    def along(x, pairs):
        return lax.ppermute(x, "col", [(2 * a + c, 2 * b + c) for a, b in pairs for c in range(2)])

    def after(x, *earlier):
        return lax.optimization_barrier((x, *earlier))[0]

    def local(amplitudes, intermediate):
        kk, occ, cs, v = amplitudes.shape
        ai = occ // nrow
        vs = v // ncol
        rows = ai * vs
        row = lax.axis_index("row").reshape(1)
        col = lax.axis_index("col")
        z, core = col // 2, (col % 2).reshape(1)
        end = (z == 0) | (z == nz - 1)

        w = intermediate.reshape(kk * v, v)
        line = nz == 4
        own = (w, across(w))
        if line:
            swap = [(1, 2), (2, 1)]
            outward = [(1, 0), (2, 3)]
            x1 = along(w, [(a, a ^ 1) for a in range(nz)])
            y2 = along(w, swap)
            pair1 = (x1, across(x1))
            own = (w, after(own[1], pair1[1]))

        blocks = pl.pallas_call(
            functools.partial(spread_kernel, nrow, ncol),
            out_shape=jax.ShapeDtypeStruct((ncol, kk, cs, occ * vs), BF16),
            in_specs=[SMEM, VMEM],
            out_specs=VMEM,
            compiler_params=PARAMS,
        )(row, amplitudes)
        raw = lax.all_to_all(blocks, "col", 0, 0, tiled=True)
        sent = [jax.ShapeDtypeStruct((2, rows, v), BF16)] * (nrow - 1)
        sent = [jax.ShapeDtypeStruct((2, rows, v), F32)] + sent
        panel, *parts = pl.pallas_call(
            first_product_kernel,
            out_shape=[jax.ShapeDtypeStruct((nrow * rows, kk * v), BF16)] + sent,
            in_specs=[SMEM] + [VMEM] * 3,
            out_specs=[VMEM] * (1 + nrow),
            compiler_params=PARAMS,
        )(core, raw, *own)

        def product(pair):
            return pl.pallas_call(
                functools.partial(product_kernel, 1),
                out_shape=sent,
                in_specs=[SMEM] + [VMEM] * 3,
                out_specs=[VMEM] * nrow,
                compiler_params=PARAMS,
            )(core, panel, *pair)

        def exchange(parts):
            sent = {}
            for t in range(len(parts) - 1, 0, -1):
                sent[t] = lax.ppermute(parts[t], "row", [(r, r ^ t) for r in range(nrow)])
            return [parts[0]] + [sent[t] for t in range(1, len(parts))]

        def summed(group):
            total = group[0]
            for part in group[1:]:
                total = total + part.astype(F32)
            return total.astype(BF16)

        if line:
            x1, y2, blocks = lax.optimization_barrier((x1, y2, blocks))
            y3, e2 = along(x1, swap), along(y2, outward)
            sums = [summed(exchange(parts))]
            parts = product(pair1)
            far = [(r, r ^ (nrow - 1)) for r in range(nrow)]
            lead = lax.ppermute(parts[-1][:1], "row", far)
            rest = lax.ppermute(parts[-1][1:], "row", far)
            e3 = along(after(y3, sums[0], lead), outward)
            sums.append(summed(exchange(parts[:-1]) + [jnp.concatenate([lead, rest])]))
            x2 = jnp.where(end, e2, y2)
            group = exchange(product((after(x2, sums[1]), across(x2))))
            sums.append(summed(group))
            x3 = jnp.where(end, after(e3, *group[nrow // 2 :]), y3)
            last = exchange(product((x3, across(x3))))
            last = [last[0]] + last[:0:-1]
            slots = [z, z ^ 1, jnp.where(end, z ^ 2, 3 - z), jnp.where(end, 3 - z, z ^ 2)]
        else:
            last = exchange(parts)
            sums = []
            for m in range(1, nz):
                sums.append(summed(last))
                x = along(w, [(a, a ^ m) for a in range(nz)])
                last = exchange(product((after(x, sums[-1]), across(x))))
            slots = [z ^ m for m in range(nz)]
        groups = [[x] for x in sums] + [last]

        sizes = [len(g) for g in groups]
        first, turned = pl.pallas_call(
            functools.partial(turn_kernel, sizes, ncol),
            out_shape=[
                jax.ShapeDtypeStruct((occ, rows, v), BF16),
                jax.ShapeDtypeStruct((nrow * ncol, ai, vs, rows), BF16),
            ],
            in_specs=[SMEM] + [VMEM] * sum(sizes),
            out_specs=[VMEM] * 2,
            compiler_params=PARAMS,
        )(jnp.stack(slots).astype(jnp.int32), *[x for g in groups for x in g])
        second = lax.all_to_all(turned, ("row", "col"), 0, 0, tiled=True)

        return pl.pallas_call(
            functools.partial(final_kernel, nrow, ncol),
            out_shape=jax.ShapeDtypeStruct((ai, occ, vs, v), BF16),
            in_specs=[VMEM] * 2,
            out_specs=VMEM,
            compiler_params=PARAMS,
        )(first, second)

    placed = P("row", None, "col", None)
    return jax.shard_map(
        local, mesh=mesh, in_specs=(placed, placed), out_specs=placed, check_vma=False
    )
```

```python
import functools

import jax
import jax.numpy as jnp
from jax import lax
from jax.experimental import pallas as pl
from jax.experimental.pallas import tpu as pltpu
from jax.sharding import PartitionSpec as P

F32, BF16 = jnp.float32, jnp.bfloat16
VMEM = pl.BlockSpec(memory_space=pltpu.VMEM)
SMEM = pl.BlockSpec(memory_space=pltpu.SMEM)
PARAMS = pltpu.CompilerParams(vmem_limit_bytes=16 * 1024 * 1024)


def spread_kernel(nrow, ncol, row_ref, a_ref, out_ref):
    kk, occ, _, v = a_ref.shape
    ai, vs = occ // nrow, v // ncol
    for k in range(kk):
        tiles = [a_ref[k, (row_ref[0] ^ t) * ai + i] for t in range(nrow) for i in range(ai)]
        for s in range(ncol):
            piece = [tile[:, s * vs : (s + 1) * vs] for tile in tiles]
            out_ref[s, k] = jnp.concatenate(piece, axis=1)


def product_kernel(sets, core_ref, panel_ref, *refs):
    core = core_ref[0]
    blocks, outs = refs[: 2 * sets], refs[2 * sets :]
    size = len(outs) // sets
    rows = outs[0].shape[1]
    for m in range(sets):
        to = outs[m * size : (m + 1) * size]
        for c in range(2):
            prod = jnp.dot(panel_ref[...], blocks[2 * m + c][...], preferred_element_type=F32)
            to[0][core ^ c] = prod[:rows]
            for t in range(1, size):
                to[t][core ^ c] = prod[t * rows : (t + 1) * rows].astype(BF16)


def first_product_kernel(core_ref, raw_ref, here_ref, there_ref, panel_ref, *outs):
    ncol, kk, cs, wide = raw_ref.shape
    v = ncol * cs
    for k in range(kk):
        part = raw_ref[:, k].reshape(v, wide)
        panel_ref[:, k * v : (k + 1) * v] = part.T
    product_kernel(1, core_ref, panel_ref, here_ref, there_ref, *outs)


def turn_kernel(sizes, ncol, slot_ref, *refs):
    first_ref, turned_ref = refs[-2:]
    vs = turned_ref.shape[2]
    at = 0
    for size in sizes:
        parts, refs = refs[:size], refs[size:]
        for m in range(parts[0].shape[0] // 2):
            slot = slot_ref[at]
            at += 1
            for p in range(2):
                total = parts[0][2 * m + p]
                for other in parts[1:]:
                    total = total + other[2 * m + p].astype(F32)
                total = total.astype(BF16)
                first_ref[2 * slot + p] = total
                turned = total.astype(F32).T.astype(BF16)
                for s in range(ncol):
                    turned_ref[slot * ncol + s, p] = turned[s * vs : (s + 1) * vs]


def final_kernel(nrow, ncol, first_ref, second_ref, out_ref):
    ai, _, vs, _ = out_ref.shape
    for i in range(ai):
        for r in range(nrow):
            tiles = [second_ref[r * ncol + s, i].astype(F32) for s in range(ncol)]
            for q in range(ai):
                second = jnp.concatenate([x[:, q * vs : (q + 1) * vs] for x in tiles], axis=1)
                first = first_ref[r * ai + q, i * vs : (i + 1) * vs, :].astype(F32)
                out_ref[i, r * ai + q] = (first + second).astype(BF16)


def solution(mesh):
    nrow, ncol = mesh.shape["row"], mesh.shape["col"]
    nz = ncol // 2

    def across(x):
        return lax.ppermute(x, "col", [(s, s ^ 1) for s in range(ncol)])

    def along(x, pairs):
        return lax.ppermute(x, "col", [(2 * a + c, 2 * b + c) for a, b in pairs for c in range(2)])

    def after(x, *earlier):
        return lax.optimization_barrier((x, *earlier))[0]

    def local(amplitudes, intermediate):
        kk, occ, cs, v = amplitudes.shape
        ai = occ // nrow
        vs = v // ncol
        rows = ai * vs
        row = lax.axis_index("row").reshape(1)
        col = lax.axis_index("col")
        z, core = col // 2, (col % 2).reshape(1)
        end = (z == 0) | (z == nz - 1)

        w = intermediate.reshape(kk * v, v)
        line = nz == 4
        own = (w, across(w))
        if line:
            swap = [(1, 2), (2, 1)]
            outward = [(1, 0), (2, 3)]
            x1 = along(w, [(a, a ^ 1) for a in range(nz)])
            y2 = along(w, swap)
            pair1 = (x1, across(x1))
            own = (w, after(own[1], pair1[1]))

        blocks = pl.pallas_call(
            functools.partial(spread_kernel, nrow, ncol),
            out_shape=jax.ShapeDtypeStruct((ncol, kk, cs, occ * vs), BF16),
            in_specs=[SMEM, VMEM],
            out_specs=VMEM,
            compiler_params=PARAMS,
        )(row, amplitudes)
        raw = lax.all_to_all(blocks, "col", 0, 0, tiled=True)
        sent = [jax.ShapeDtypeStruct((2, rows, v), BF16)] * (nrow - 1)
        sent = [jax.ShapeDtypeStruct((2, rows, v), F32)] + sent
        panel, *parts = pl.pallas_call(
            first_product_kernel,
            out_shape=[jax.ShapeDtypeStruct((nrow * rows, kk * v), BF16)] + sent,
            in_specs=[SMEM] + [VMEM] * 3,
            out_specs=[VMEM] * (1 + nrow),
            compiler_params=PARAMS,
        )(core, raw, *own)

        def product(pair):
            return pl.pallas_call(
                functools.partial(product_kernel, 1),
                out_shape=sent,
                in_specs=[SMEM] + [VMEM] * 3,
                out_specs=[VMEM] * nrow,
                compiler_params=PARAMS,
            )(core, panel, *pair)

        def exchange(parts):
            sent = {}
            for t in range(nrow - 1, 0, -1):
                sent[t] = lax.ppermute(parts[t], "row", [(r, r ^ t) for r in range(nrow)])
            return [parts[0]] + [sent[t] for t in range(1, nrow)]

        def summed(group):
            total = group[0]
            for part in group[1:]:
                total = total + part.astype(F32)
            return total.astype(BF16)

        if line:
            x1, y2, blocks = lax.optimization_barrier((x1, y2, blocks))
            y3, e2 = along(x1, swap), along(y2, outward)
            sums = [summed(exchange(parts))]
            parts = product(pair1)
            group = exchange(parts)
            e3 = along(after(y3, sums[0], group[-1]), outward)
            sums.append(summed(group))
            x2 = jnp.where(end, e2, y2)
            group = exchange(product((after(x2, sums[1]), across(x2))))
            sums.append(summed(group))
            x3 = jnp.where(end, after(e3, group[-1]), y3)
            last = exchange(product((x3, across(x3))))
            last = [last[0]] + last[:0:-1]
            slots = [z, z ^ 1, jnp.where(end, z ^ 2, 3 - z), jnp.where(end, 3 - z, z ^ 2)]
        else:
            last = exchange(parts)
            sums = []
            for m in range(1, nz):
                sums.append(summed(last))
                x = along(w, [(a, a ^ m) for a in range(nz)])
                last = exchange(product((after(x, sums[-1]), across(x))))
            slots = [z ^ m for m in range(nz)]
        groups = [[x] for x in sums] + [last]

        sizes = [len(g) for g in groups]
        first, turned = pl.pallas_call(
            functools.partial(turn_kernel, sizes, ncol),
            out_shape=[
                jax.ShapeDtypeStruct((occ, rows, v), BF16),
                jax.ShapeDtypeStruct((nrow * ncol, ai, vs, rows), BF16),
            ],
            in_specs=[SMEM] + [VMEM] * sum(sizes),
            out_specs=[VMEM] * 2,
            compiler_params=PARAMS,
        )(jnp.stack(slots).astype(jnp.int32), *[x for g in groups for x in g])
        second = lax.all_to_all(turned, ("row", "col"), 0, 0, tiled=True)

        return pl.pallas_call(
            functools.partial(final_kernel, nrow, ncol),
            out_shape=jax.ShapeDtypeStruct((ai, occ, vs, v), BF16),
            in_specs=[VMEM] * 2,
            out_specs=VMEM,
            compiler_params=PARAMS,
        )(first, second)

    placed = P("row", None, "col", None)
    return jax.shard_map(
        local, mesh=mesh, in_specs=(placed, placed), out_specs=placed, check_vma=False
    )
```

```python
import functools

import jax
import jax.numpy as jnp
from jax import lax
from jax.experimental import pallas as pl
from jax.experimental.pallas import tpu as pltpu
from jax.sharding import PartitionSpec as P

F32, BF16 = jnp.float32, jnp.bfloat16
VMEM = pl.BlockSpec(memory_space=pltpu.VMEM)
SMEM = pl.BlockSpec(memory_space=pltpu.SMEM)
PARAMS = pltpu.CompilerParams(vmem_limit_bytes=16 * 1024 * 1024)


def spread_kernel(nrow, ncol, row_ref, a_ref, out_ref):
    kk, occ, _, v = a_ref.shape
    ai, vs = occ // nrow, v // ncol
    for k in range(kk):
        tiles = [a_ref[k, (row_ref[0] ^ t) * ai + i] for t in range(nrow) for i in range(ai)]
        for s in range(ncol):
            piece = [tile[:, s * vs : (s + 1) * vs] for tile in tiles]
            out_ref[s, k] = jnp.concatenate(piece, axis=1)


def product_kernel(sets, core_ref, panel_ref, *refs):
    core = core_ref[0]
    blocks, outs = refs[: 2 * sets], refs[2 * sets :]
    size = len(outs) // sets
    rows = outs[0].shape[1]
    for m in range(sets):
        to = outs[m * size : (m + 1) * size]
        for c in range(2):
            prod = jnp.dot(panel_ref[...], blocks[2 * m + c][...], preferred_element_type=F32)
            to[0][core ^ c] = prod[:rows]
            for t in range(1, size):
                to[t][core ^ c] = prod[t * rows : (t + 1) * rows].astype(BF16)


def first_product_kernel(core_ref, raw_ref, here_ref, there_ref, panel_ref, *outs):
    ncol, kk, cs, wide = raw_ref.shape
    v = ncol * cs
    for k in range(kk):
        part = raw_ref[:, k].reshape(v, wide)
        panel_ref[:, k * v : (k + 1) * v] = part.T
    product_kernel(1, core_ref, panel_ref, here_ref, there_ref, *outs)


def turn_kernel(sizes, ncol, slot_ref, *refs):
    first_ref, turned_ref = refs[-2:]
    vs = turned_ref.shape[2]
    at = 0
    for size in sizes:
        parts, refs = refs[:size], refs[size:]
        for m in range(parts[0].shape[0] // 2):
            slot = slot_ref[at]
            at += 1
            for p in range(2):
                total = parts[0][2 * m + p]
                for other in parts[1:]:
                    total = total + other[2 * m + p].astype(F32)
                total = total.astype(BF16)
                first_ref[2 * slot + p] = total
                turned = total.astype(F32).T.astype(BF16)
                for s in range(ncol):
                    turned_ref[slot * ncol + s, p] = turned[s * vs : (s + 1) * vs]


def final_kernel(nrow, ncol, first_ref, second_ref, out_ref):
    ai, _, vs, _ = out_ref.shape
    for i in range(ai):
        for r in range(nrow):
            tiles = [second_ref[r * ncol + s, i].astype(F32) for s in range(ncol)]
            for q in range(ai):
                second = jnp.concatenate([x[:, q * vs : (q + 1) * vs] for x in tiles], axis=1)
                first = first_ref[r * ai + q, i * vs : (i + 1) * vs, :].astype(F32)
                out_ref[i, r * ai + q] = (first + second).astype(BF16)


def solution(mesh):
    nrow, ncol = mesh.shape["row"], mesh.shape["col"]
    nz = ncol // 2

    def across(x):
        return lax.ppermute(x, "col", [(s, s ^ 1) for s in range(ncol)])

    def along(x, pairs):
        return lax.ppermute(x, "col", [(2 * a + c, 2 * b + c) for a, b in pairs for c in range(2)])

    def after(x, *earlier):
        return lax.optimization_barrier((x, *earlier))[0]

    def local(amplitudes, intermediate):
        kk, occ, cs, v = amplitudes.shape
        ai = occ // nrow
        vs = v // ncol
        rows = ai * vs
        row = lax.axis_index("row").reshape(1)
        col = lax.axis_index("col")
        z, core = col // 2, (col % 2).reshape(1)
        end = (z == 0) | (z == nz - 1)

        w = intermediate.reshape(kk * v, v)
        line = nz == 4
        own = (w, across(w))
        if line:
            swap = [(1, 2), (2, 1)]
            outward = [(1, 0), (2, 3)]
            x1 = along(w, [(a, a ^ 1) for a in range(nz)])
            y2 = along(w, swap)
            pair1 = (x1, across(x1))
            own = (w, after(own[1], pair1[1]))

        blocks = pl.pallas_call(
            functools.partial(spread_kernel, nrow, ncol),
            out_shape=jax.ShapeDtypeStruct((ncol, kk, cs, occ * vs), BF16),
            in_specs=[SMEM, VMEM],
            out_specs=VMEM,
            compiler_params=PARAMS,
        )(row, amplitudes)
        raw = lax.all_to_all(blocks, "col", 0, 0, tiled=True)
        sent = [jax.ShapeDtypeStruct((2, rows, v), BF16)] * (nrow - 1)
        sent = [jax.ShapeDtypeStruct((2, rows, v), F32)] + sent
        panel, *parts = pl.pallas_call(
            first_product_kernel,
            out_shape=[jax.ShapeDtypeStruct((nrow * rows, kk * v), BF16)] + sent,
            in_specs=[SMEM] + [VMEM] * 3,
            out_specs=[VMEM] * (1 + nrow),
            compiler_params=PARAMS,
        )(core, raw, *own)

        def product(pair):
            return pl.pallas_call(
                functools.partial(product_kernel, 1),
                out_shape=sent,
                in_specs=[SMEM] + [VMEM] * 3,
                out_specs=[VMEM] * nrow,
                compiler_params=PARAMS,
            )(core, panel, *pair)

        def exchange(parts):
            sent = {}
            for t in range(nrow - 1, 0, -1):
                sent[t] = lax.ppermute(parts[t], "row", [(r, r ^ t) for r in range(nrow)])
            return [parts[0]] + [sent[t] for t in range(1, nrow)]

        def summed(group):
            total = group[0]
            for part in group[1:]:
                total = total + part.astype(F32)
            return total.astype(BF16)

        if line:
            x1, y2, blocks = lax.optimization_barrier((x1, y2, blocks))
            y3, e2 = along(x1, swap), along(y2, outward)
            sums = [summed(exchange(parts))]
            parts = product(pair1)
            group = exchange(parts)
            e3 = along(after(y3, sums[0], group[-1]), outward)
            sums.append(summed(group))
            x2 = jnp.where(end, e2, y2)
            group = exchange(product((after(x2, *group[1:]), across(x2))))
            sums.append(summed(group))
            x3 = jnp.where(end, after(e3, group[-1]), y3)
            last = exchange(product((x3, across(x3))))
            last = [last[0]] + last[:0:-1]
            slots = [z, z ^ 1, jnp.where(end, z ^ 2, 3 - z), jnp.where(end, 3 - z, z ^ 2)]
        else:
            last = exchange(parts)
            sums = []
            for m in range(1, nz):
                sums.append(summed(last))
                x = along(w, [(a, a ^ m) for a in range(nz)])
                last = exchange(product((after(x, sums[-1]), across(x))))
            slots = [z ^ m for m in range(nz)]
        groups = [[x] for x in sums] + [last]

        sizes = [len(g) for g in groups]
        first, turned = pl.pallas_call(
            functools.partial(turn_kernel, sizes, ncol),
            out_shape=[
                jax.ShapeDtypeStruct((occ, rows, v), BF16),
                jax.ShapeDtypeStruct((nrow * ncol, ai, vs, rows), BF16),
            ],
            in_specs=[SMEM] + [VMEM] * sum(sizes),
            out_specs=[VMEM] * 2,
            compiler_params=PARAMS,
        )(jnp.stack(slots).astype(jnp.int32), *[x for g in groups for x in g])
        second = lax.all_to_all(turned, ("row", "col"), 0, 0, tiled=True)

        return pl.pallas_call(
            functools.partial(final_kernel, nrow, ncol),
            out_shape=jax.ShapeDtypeStruct((ai, occ, vs, v), BF16),
            in_specs=[VMEM] * 2,
            out_specs=VMEM,
            compiler_params=PARAMS,
        )(first, second)

    placed = P("row", None, "col", None)
    return jax.shard_map(
        local, mesh=mesh, in_specs=(placed, placed), out_specs=placed, check_vma=False
    )
```

```python
import functools

import jax
import jax.numpy as jnp
from jax import lax
from jax.experimental import pallas as pl
from jax.experimental.pallas import tpu as pltpu
from jax.sharding import PartitionSpec as P

F32, BF16 = jnp.float32, jnp.bfloat16
VMEM = pl.BlockSpec(memory_space=pltpu.VMEM)
SMEM = pl.BlockSpec(memory_space=pltpu.SMEM)
PARAMS = pltpu.CompilerParams(vmem_limit_bytes=16 * 1024 * 1024)


def spread_kernel(nrow, ncol, row_ref, a_ref, out_ref):
    kk, occ, _, v = a_ref.shape
    ai, vs = occ // nrow, v // ncol
    for k in range(kk):
        tiles = [a_ref[k, (row_ref[0] ^ t) * ai + i] for t in range(nrow) for i in range(ai)]
        for s in range(ncol):
            piece = [tile[:, s * vs : (s + 1) * vs] for tile in tiles]
            out_ref[s, k] = jnp.concatenate(piece, axis=1)


def product_kernel(sets, core_ref, panel_ref, *refs):
    core = core_ref[0]
    blocks, outs = refs[: 2 * sets], refs[2 * sets :]
    size = len(outs) // sets
    rows = outs[0].shape[1]
    for m in range(sets):
        to = outs[m * size : (m + 1) * size]
        for c in range(2):
            prod = jnp.dot(panel_ref[...], blocks[2 * m + c][...], preferred_element_type=F32)
            to[0][core ^ c] = prod[:rows]
            for t in range(1, size):
                to[t][core ^ c] = prod[t * rows : (t + 1) * rows].astype(BF16)


def first_product_kernel(core_ref, raw_ref, here_ref, there_ref, panel_ref, *outs):
    ncol, kk, cs, wide = raw_ref.shape
    v = ncol * cs
    for k in range(kk):
        part = raw_ref[:, k].reshape(v, wide)
        panel_ref[:, k * v : (k + 1) * v] = part.T
    product_kernel(1, core_ref, panel_ref, here_ref, there_ref, *outs)


def turn_kernel(sizes, ncol, slot_ref, *refs):
    first_ref, turned_ref = refs[-2:]
    vs = turned_ref.shape[2]
    at = 0
    for size in sizes:
        parts, refs = refs[:size], refs[size:]
        for m in range(parts[0].shape[0] // 2):
            slot = slot_ref[at]
            at += 1
            for p in range(2):
                total = parts[0][2 * m + p]
                for other in parts[1:]:
                    total = total + other[2 * m + p].astype(F32)
                total = total.astype(BF16)
                first_ref[2 * slot + p] = total
                turned = total.astype(F32).T.astype(BF16)
                for s in range(ncol):
                    turned_ref[slot * ncol + s, p] = turned[s * vs : (s + 1) * vs]


def final_kernel(nrow, ncol, first_ref, second_ref, out_ref):
    ai, _, vs, _ = out_ref.shape
    for i in range(ai):
        for r in range(nrow):
            tiles = [second_ref[r * ncol + s, i].astype(F32) for s in range(ncol)]
            for q in range(ai):
                second = jnp.concatenate([x[:, q * vs : (q + 1) * vs] for x in tiles], axis=1)
                first = first_ref[r * ai + q, i * vs : (i + 1) * vs, :].astype(F32)
                out_ref[i, r * ai + q] = (first + second).astype(BF16)


def solution(mesh):
    nrow, ncol = mesh.shape["row"], mesh.shape["col"]
    nz = ncol // 2

    def across(x):
        return lax.ppermute(x, "col", [(s, s ^ 1) for s in range(ncol)])

    def along(x, pairs):
        return lax.ppermute(x, "col", [(2 * a + c, 2 * b + c) for a, b in pairs for c in range(2)])

    def after(x, *earlier):
        return lax.optimization_barrier((x, *earlier))[0]

    def local(amplitudes, intermediate):
        kk, occ, cs, v = amplitudes.shape
        ai = occ // nrow
        vs = v // ncol
        rows = ai * vs
        row = lax.axis_index("row").reshape(1)
        col = lax.axis_index("col")
        z, core = col // 2, (col % 2).reshape(1)
        end = (z == 0) | (z == nz - 1)

        w = intermediate.reshape(kk * v, v)
        line = nz == 4
        own = (w, across(w))
        if line:
            swap = [(1, 2), (2, 1)]
            outward = [(1, 0), (2, 3)]
            x1 = along(w, [(a, a ^ 1) for a in range(nz)])
            y2 = along(w, swap)
            pair1 = (x1, across(x1))
            own = (w, after(own[1], pair1[1]))

        blocks = pl.pallas_call(
            functools.partial(spread_kernel, nrow, ncol),
            out_shape=jax.ShapeDtypeStruct((ncol, kk, cs, occ * vs), BF16),
            in_specs=[SMEM, VMEM],
            out_specs=VMEM,
            compiler_params=PARAMS,
        )(row, amplitudes)
        raw = lax.all_to_all(blocks, "col", 0, 0, tiled=True)
        sent = [jax.ShapeDtypeStruct((2, rows, v), BF16)] * (nrow - 1)
        sent = [jax.ShapeDtypeStruct((2, rows, v), F32)] + sent
        panel, *parts = pl.pallas_call(
            first_product_kernel,
            out_shape=[jax.ShapeDtypeStruct((nrow * rows, kk * v), BF16)] + sent,
            in_specs=[SMEM] + [VMEM] * 3,
            out_specs=[VMEM] * (1 + nrow),
            compiler_params=PARAMS,
        )(core, raw, *own)

        def product(pair):
            return pl.pallas_call(
                functools.partial(product_kernel, 1),
                out_shape=sent,
                in_specs=[SMEM] + [VMEM] * 3,
                out_specs=[VMEM] * nrow,
                compiler_params=PARAMS,
            )(core, panel, *pair)

        def exchange(parts):
            sent = {}
            for t in range(nrow - 1, 0, -1):
                sent[t] = lax.ppermute(parts[t], "row", [(r, r ^ t) for r in range(nrow)])
            return [parts[0]] + [sent[t] for t in range(1, nrow)]

        def summed(group):
            total = group[0]
            for part in group[1:]:
                total = total + part.astype(F32)
            return total.astype(BF16)

        if line:
            x1, y2, blocks = lax.optimization_barrier((x1, y2, blocks))
            y3, e2 = along(x1, swap), along(y2, outward)
            group0 = exchange(parts)
            sums = [summed(group0)]
            parts = product(pair1)
            group = exchange(parts)
            e3 = along(after(y3, *group0[1:], group[-1]), outward)
            sums.append(summed(group))
            x2 = jnp.where(end, e2, y2)
            group = exchange(product((after(x2, *group[1:]), across(x2))))
            sums.append(summed(group))
            x3 = jnp.where(end, after(e3, group[-1]), y3)
            last = exchange(product((x3, across(x3))))
            last = [last[0]] + last[:0:-1]
            slots = [z, z ^ 1, jnp.where(end, z ^ 2, 3 - z), jnp.where(end, 3 - z, z ^ 2)]
        else:
            last = exchange(parts)
            sums = []
            for m in range(1, nz):
                sums.append(summed(last))
                x = along(w, [(a, a ^ m) for a in range(nz)])
                last = exchange(product((after(x, sums[-1]), across(x))))
            slots = [z ^ m for m in range(nz)]
        groups = [[x] for x in sums] + [last]

        sizes = [len(g) for g in groups]
        first, turned = pl.pallas_call(
            functools.partial(turn_kernel, sizes, ncol),
            out_shape=[
                jax.ShapeDtypeStruct((occ, rows, v), BF16),
                jax.ShapeDtypeStruct((nrow * ncol, ai, vs, rows), BF16),
            ],
            in_specs=[SMEM] + [VMEM] * sum(sizes),
            out_specs=[VMEM] * 2,
            compiler_params=PARAMS,
        )(jnp.stack(slots).astype(jnp.int32), *[x for g in groups for x in g])
        second = lax.all_to_all(turned, ("row", "col"), 0, 0, tiled=True)

        return pl.pallas_call(
            functools.partial(final_kernel, nrow, ncol),
            out_shape=jax.ShapeDtypeStruct((ai, occ, vs, v), BF16),
            in_specs=[VMEM] * 2,
            out_specs=VMEM,
            compiler_params=PARAMS,
        )(first, second)

    placed = P("row", None, "col", None)
    return jax.shard_map(
        local, mesh=mesh, in_specs=(placed, placed), out_specs=placed, check_vma=False
    )
```
